256 devices in a mesh: seq: 64 (over y_hi, x, z), head: 4 (over y_lo, core).
Axes of the slice: x: 4, y: 4 (y_hi: 2, y_lo: 2; y = y_hi * 2 + y_lo), z: 8, core: 2. Of those that a mesh axis runs over, the one named last changes fastest.
Arguments:
- video_query: bfloat16 [16384, 2048], P('seq', 'head'), may hold values from -360 to 360
- video_key: bfloat16 [16384, 2048], P('seq', 'head'), may hold values from -6 to 6
- video_value: bfloat16 [16384, 2048], P('seq', 'head'), may hold values from -6 to 6
- audio_query: bfloat16 [2048, 2048], P('seq', 'head'), may hold values from -360 to 360
- audio_key: bfloat16 [2048, 2048], P('seq', 'head'), may hold values from -6 to 6
- audio_value: bfloat16 [2048, 2048], P('seq', 'head'), may hold values from -6 to 6
- window_start: int32 [128], replicated, may hold values from 0 to 48, as said below
- video_out_weight: bfloat16 [2048, 4096], P('head'), may hold values from -0.125 to 0.125
- audio_out_weight: bfloat16 [2048, 2048], P('head'), may hold values from -0.125 to 0.125
Outputs:
- video_mixed: bfloat16 [16384, 4096], P(('seq', 'head'))
- audio_mixed: bfloat16 [2048, 2048], P(('seq', 'head'))
The draws below stay inside these ranges and needn't reach their ends.
Inputs may be any that keep to these rules, and one draw needn't show every extreme that they name: Video block i (tokens i * 128 to (i + 1) * 128 - 1) is aligned with the 80 audio blocks of 16 tokens from window_start[i] on; every audio block is aligned with some video block.
All inputs are finite; a program needn't handle non-finite values.
Results may differ from the reference program's by a relative error of at most 0.02.
Values may be sent and summed in bfloat16 or wider, within the bound.
A program may use at most 128 MiB of HBM per device.

```python
import jax
import jax.numpy as jnp
from jax import lax

DV = 4096
DA = 2048
HEADS = 16
HEAD_DIM = 128
VBLOCK = 128
ABLOCK = 16
VID_TOK = 16384
AUD_TOK = 2048
NVB = 128
NAB = 128
WIN = 80
INNER = 2048


def normal_rows(key, row_count, limit):
    return jnp.clip(jax.random.normal(key, (row_count, INNER), jnp.float32), -limit, limit)


def draw_video_query(key, part):
    key = jax.random.fold_in(key, 1)
    first_key = jax.random.fold_in(key, 0)
    values = normal_rows(first_key, VID_TOK, 6.0)
    return values.astype(jnp.bfloat16)


def draw_audio_query(key, part):
    key = jax.random.fold_in(key, 2)
    first_key = jax.random.fold_in(key, 0)
    values = normal_rows(first_key, AUD_TOK, 6.0)
    return values.astype(jnp.bfloat16)


def draw_video_key(key, part):
    key = jax.random.fold_in(key, 3)
    first_key = jax.random.fold_in(key, 0)
    values = normal_rows(first_key, VID_TOK, 6.0)
    return values.astype(jnp.bfloat16)


def draw_audio_key(key, part):
    key = jax.random.fold_in(key, 4)
    first_key = jax.random.fold_in(key, 0)
    values = normal_rows(first_key, AUD_TOK, 6.0)
    return values.astype(jnp.bfloat16)


def draw_window_start(key, part):
    key = jax.random.fold_in(key, 5)
    block_ids = jnp.arange(NVB, dtype=jnp.int32)
    center = block_ids * NAB // NVB
    jitter = jax.random.randint(key, (NVB,), -1, 2, jnp.int32)
    return jnp.clip(center - WIN // 2 + jitter, 0, NAB - WIN).astype(jnp.int32)


def shard_levels(rng, extent, cuts, smallest, high):
    loudness, own = 1.0, jax.random.fold_in(rng, 6)
    for axis_at, parts in cuts:
        heights = jnp.exp(jax.random.uniform(jax.random.fold_in(own, axis_at), (parts,), jnp.float32, smallest / len(cuts), high / len(cuts)))
        loudness = loudness * jnp.repeat(heights, extent[axis_at] // parts).reshape([-1 if axis == axis_at else 1 for axis in range(len(extent))])
    return loudness


def bell_draw(rng, extent, spread, reach, cuts=(), held_as=jnp.bfloat16):
    drawn = spread * jax.random.normal(rng, extent, jnp.float32)
    if cuts:
        drawn = drawn * shard_levels(rng, extent, cuts, -0.22, 0.18)
    return jnp.clip(drawn, -reach, reach).astype(held_as)


def setup_inputs(seed: int = 0) -> dict:
    streams_of = jax.random.split(jax.random.key(seed), 10)
    return {
        "video_query": draw_video_query(jax.random.fold_in(streams_of[9], 71), 0),
        "video_key": draw_video_key(jax.random.fold_in(streams_of[9], 71), 0),
        "video_value": bell_draw(streams_of[2], (VID_TOK, INNER), 1.0, 6.0, ((0, 64), (1, 4))),
        "audio_query": draw_audio_query(jax.random.fold_in(streams_of[9], 71), 0),
        "audio_key": draw_audio_key(jax.random.fold_in(streams_of[9], 71), 0),
        "audio_value": bell_draw(streams_of[5], (AUD_TOK, INNER), 1.0, 6.0, ((0, 64), (1, 4))),
        "window_start": draw_window_start(jax.random.fold_in(streams_of[9], 71), 0),
        "video_out_weight": bell_draw(streams_of[7], (INNER, DV), INNER ** -0.5, 0.125, ((0, 4),)),
        "audio_out_weight": bell_draw(streams_of[8], (INNER, DA), INNER ** -0.5, 0.125, ((0, 4),)),
    }


def soft_attend(head_query, head_key, head_value, keep_mask):
    scores = jnp.dot(head_query, head_key.T, preferred_element_type=jnp.float32) * (HEAD_DIM ** -0.5)
    masked = jnp.where(keep_mask, scores, -jnp.inf)
    row_top = jnp.max(masked, axis=1, keepdims=True)
    weights = jnp.where(keep_mask, jnp.exp(masked - row_top), 0.0)
    total = jnp.sum(weights, axis=1, keepdims=True)
    numerator = jnp.dot(weights.astype(jnp.bfloat16), head_value, preferred_element_type=jnp.float32)
    return numerator / total


def block_attend(query, key_rows, value_rows, allowed_fn):
    row_count = query.shape[0]
    block_rows = min(512, row_count)
    key_index = jnp.arange(key_rows.shape[0], dtype=jnp.int32)

    def one_block(block_index):
        first_row = (block_index * block_rows).astype(jnp.int32)
        row_index = first_row + jnp.arange(block_rows, dtype=jnp.int32)
        keep_mask = allowed_fn(row_index, key_index)
        query_rows = lax.dynamic_slice_in_dim(query, first_row, block_rows, 0)

        def one_head(head_index):
            offset = (head_index * HEAD_DIM).astype(jnp.int32)
            head_query = lax.dynamic_slice_in_dim(query_rows, offset, HEAD_DIM, 1)
            head_key = lax.dynamic_slice_in_dim(key_rows, offset, HEAD_DIM, 1)
            head_value = lax.dynamic_slice_in_dim(value_rows, offset, HEAD_DIM, 1)
            return soft_attend(head_query, head_key, head_value, keep_mask)

        heads_out = lax.map(one_head, jnp.arange(HEADS, dtype=jnp.int32))
        return heads_out.transpose(1, 0, 2).reshape(block_rows, HEADS * HEAD_DIM)

    blocks = lax.map(one_block, jnp.arange(row_count // block_rows, dtype=jnp.int32))
    return blocks.reshape(row_count, HEADS * HEAD_DIM).astype(jnp.bfloat16)


def reference(video_query, video_key, video_value, audio_query, audio_key, audio_value, window_start, video_out_weight, audio_out_weight):
    start_tokens = jnp.repeat(window_start, VBLOCK)

    def video_allowed(row_index, key_index):
        first_block = start_tokens[row_index][:, None]
        audio_block = (key_index // ABLOCK)[None, :]
        return (audio_block >= first_block) & (audio_block < first_block + WIN)

    def audio_allowed(row_index, key_index):
        first_block = start_tokens[key_index][None, :]
        audio_block = (row_index // ABLOCK)[:, None]
        return (audio_block >= first_block) & (audio_block < first_block + WIN)

    video_attention = block_attend(video_query, audio_key, audio_value, video_allowed)
    audio_attention = block_attend(audio_query, video_key, video_value, audio_allowed)
    video_mixed = jnp.dot(video_attention, video_out_weight, preferred_element_type=jnp.float32).astype(jnp.bfloat16)
    audio_mixed = jnp.dot(audio_attention, audio_out_weight, preferred_element_type=jnp.float32).astype(jnp.bfloat16)
    return video_mixed, audio_mixed
```

```python
import math

import jax
import jax.numpy as jnp
from jax import lax
from jax.experimental import pallas as pl
from jax.experimental.pallas import tpu as pltpu
from jax.sharding import PartitionSpec as P

HD = 128
VB = 128
AB = 16
WIN = 80
NX, NZ = 4, 8
VR = 256
AR = 32
NEG = -1e30
C2 = math.log2(math.e) / math.sqrt(HD)
MESH = pl.DeviceIdType.MESH
F32, BF16 = jnp.float32, jnp.bfloat16


def dev(yh, x, z, yl, c):
    return ((yh * NX + x) * NZ + z, yl * 2 + c)


def nt(a, b):
    return lax.dot_general(a, b, (((1,), (1,)), ((), ())), preferred_element_type=F32)


def kernel(
    ws, vq_in, vk_in, vv_in, aq_in, ak_in, av_in, wv_in, wa_in, ov, oa,
    vq, vk, vv, aq, ak_flat, av_flat, wv, wa, kb, vo, va, po, pst, pr, prs, ao, aa, ysend, yrecv, yown, asend, arecv,
    s_pa, r_pa, s_pb, r_pb, s_z, r_z, s_f, r_f, s_vf, r_vf, s_w, r_w, s_vo, r_vo, s_p, r_p, s_ao, r_ao, s_y, r_y, s_ya, r_ya, l_w,
):
    seq, head = lax.axis_index("seq"), lax.axis_index("head")
    yh, x, z = seq // (NX * NZ), (seq // NZ) % NX, seq % NZ
    yl, c = head // 2, head % 2
    ak, av = (ref.reshape(2 * NX, NZ, AR, HD) for ref in (ak_flat, av_flat))
    is_self = yh == c
    core_peer = dev(yh, x, z, yl, 1 - c)
    yl_peer = dev(yh, x, z, 1 - yl, c)

    def peer(j):
        return dev(c, (x + j) % NX, z, yl, yh)

    def wait(ref, sem):
        pltpu.make_async_copy(ref, ref, sem).wait()

    own_w = [
        pltpu.make_async_copy(wv_in, wv.at[c], l_w.at[0]),
        pltpu.make_async_copy(wa_in, wa.at[c], l_w.at[1]),
    ]
    for copy in own_w:
        copy.start()

    barrier = pltpu.get_barrier_semaphore()

    def greet(device):
        pl.semaphore_signal(barrier, inc=1, device_id=device, device_id_type=MESH)

    for j in range(1, NX):
        greet(peer(j))

    @pl.when(jnp.logical_not(is_self))
    def _():
        greet(peer(0))

    for j in range(NX):
        greet(dev(1 - c, (x + j) % NX, z, yl, yh))
    for d in range(1, NZ):
        greet(dev(yh, x, (z + d) % NZ, yl, c))
    greet(core_peer)
    greet(yl_peer)
    pl.semaphore_wait(barrier, 2 * NX + NZ + 1 - is_self.astype(jnp.int32))

    def exchange(src, dst, send, recv, j):
        remote = pltpu.make_async_remote_copy(
            src_ref=src, dst_ref=dst, send_sem=send, recv_sem=recv, device_id=peer(j), device_id_type=MESH
        )
        if j:
            remote.start()
            return

        @pl.when(is_self)
        def _():
            pltpu.make_async_copy(src, dst, recv).start()

        @pl.when(jnp.logical_not(is_self))
        def _():
            remote.start()

    def cols(j):
        return pl.ds(pl.multiple_of(((x + j) % NX) * HD, HD), HD)

    here = yh * NX + x
    for j in range(NX):
        exchange(aq_in.at[:, cols(j)], aq.at[z, x], s_pa.at[0, j], r_pa.at[0, x], j)
        exchange(ak_in.at[:, cols(j)], ak.at[here, z], s_pa.at[1, j], r_pa.at[1, x], j)
        exchange(av_in.at[:, cols(j)], av.at[here, z], s_pa.at[2, j], r_pa.at[2, x], j)
    for t, (src, dst) in enumerate(((vk_in, vk.at[yh]), (vv_in, vv.at[yh]), (vq_in, vq))):
        for j in range(NX):
            exchange(src.at[:, cols(j)], dst.at[x], s_pb.at[t, j], r_pb.at[t, x], j)

    other_w = [
        pltpu.make_async_remote_copy(
            src_ref=src, dst_ref=dst.at[c], send_sem=s_w.at[t], recv_sem=r_w.at[t],
            device_id=core_peer, device_id_type=MESH,
        )
        for t, (src, dst) in enumerate(((wv_in, wv), (wa_in, wa)))
    ]
    for copy in other_w:
        copy.start()

    lane = lax.broadcasted_iota(jnp.int32, (VB, 128), 1)
    for a in range(2):
        for xs in range(NX):
            for i in range(2):
                start = ws[((a * NX + xs) * NZ + z) * 2 + i]
                inside = (lane >= start) & (lane < start + WIN)
                kb[a, xs, pl.ds(i * VB, VB), :] = jnp.where(inside, 0.0, NEG).astype(BF16)

    for xs in range(NX):
        wait(aq.at[z, xs], r_pa.at[0, xs])
        wait(ak.at[c * NX + xs, z], r_pa.at[1, xs])
        wait(av.at[c * NX + xs, z], r_pa.at[2, xs])

    half = pl.ds(c * NX, NX)
    other_half = pl.ds((1 - c) * NX, NX)

    def chunk(t, zz):
        return aq.at[zz] if t == 0 else (ak, av)[t - 1].at[half, zz]

    def forward(zz):
        for t in (1, 2):
            pltpu.make_async_remote_copy(
                src_ref=chunk(t, zz), dst_ref=chunk(t, zz), send_sem=s_f.at[t - 1, zz], recv_sem=r_f.at[t - 1, zz],
                device_id=core_peer, device_id_type=MESH,
            ).start()

    forward(z)
    sent = []
    for k in range(1, NZ // 2 + 1):
        hops = [(0, t) for t in range(3)] + [(1, t) for t in range(3)]
        if k == NZ // 2:
            hops = [(0, 0), (0, 1), (1, 2)]
        for way, t in hops:
            zz = (z - k + 1 + NZ) % NZ if way == 0 else (z + k - 1) % NZ
            to = (z + 1) % NZ if way == 0 else (z + NZ - 1) % NZ
            copy = pltpu.make_async_remote_copy(
                src_ref=chunk(t, zz), dst_ref=chunk(t, zz), send_sem=s_z.at[way, t, k - 1], recv_sem=r_z.at[way, t, k - 1],
                device_id=dev(yh, x, to, yl, c), device_id_type=MESH,
            )
            copy.start()
            sent.append(copy)
        for way, t in hops:
            zz = (z - k + NZ) % NZ if way == 0 else (z + k) % NZ
            wait(chunk(t, zz), r_z.at[way, t, k - 1])
        if k < NZ // 2:
            forward((z - k + NZ) % NZ)
            forward((z + k) % NZ)
        else:
            forward((z + k) % NZ)

    vf = []
    for t, ref in enumerate((vk, vv)):
        for xs in range(NX):
            wait(ref.at[c, xs], r_pb.at[t, xs])
        copy = pltpu.make_async_remote_copy(
            src_ref=ref.at[c], dst_ref=ref.at[c], send_sem=s_vf.at[t], recv_sem=r_vf.at[t],
            device_id=core_peer, device_id_type=MESH,
        )
        copy.start()
        vf.append(copy)
    for xs in range(NX):
        wait(vq.at[xs], r_pb.at[2, xs])

    def late(zz, carry):
        wait(ak.at[other_half, zz], r_f.at[0, zz])
        wait(av.at[other_half, zz], r_f.at[1, zz])
        return carry

    lax.fori_loop(0, NZ, late, 0)

    ones_win = jnp.ones((WIN * AB, HD), BF16)

    def video_block(n, carry):
        xs, i = n // 2, n % 2
        start = ws[((c * NX + xs) * NZ + z) * 2 + i]
        blocks = pl.ds(start, WIN)
        q = vq[xs, pl.ds(pl.multiple_of(i * VB, VB), VB), :]
        s = nt(q, ak_flat[blocks].reshape(WIN * AB, HD))
        top = jnp.max(s, axis=1, keepdims=True)
        p = jnp.exp2((s - top) * C2).astype(BF16)
        v = jnp.concatenate([av_flat[blocks].reshape(WIN * AB, HD), ones_win], axis=1)
        o = jnp.dot(p, v, preferred_element_type=F32)
        vo[xs, i] = (o[:, :HD] / o[:, HD:]).astype(BF16).reshape(2, VB // 2, HD)
        return carry

    lax.fori_loop(0, 2 * NX, video_block, 0)

    my_slot = yh * NX + x

    def vo_copy(j, k):
        return pltpu.make_async_remote_copy(
            src_ref=vo.at[(x + j) % NX, :, k], dst_ref=va.at[my_slot], send_sem=s_vo.at[j, k], recv_sem=r_vo.at[my_slot],
            device_id=dev(c, (x + j) % NX, z, yl, k), device_id_type=MESH,
        )

    for j in range(NX):
        for k in range(2):
            copy = vo_copy(j, k)
            if j:
                copy.start()
            else:
                to_self = is_self & (c == k)

                @pl.when(to_self)
                def _(k=k):
                    pltpu.make_async_copy(vo.at[x, :, k], va.at[my_slot], r_vo.at[my_slot]).start()

                @pl.when(jnp.logical_not(to_self))
                def _(copy=copy):
                    copy.start()

    for t, ref in enumerate((vk, vv)):
        wait(ref.at[1 - c], r_vf.at[t])
    row = lax.broadcasted_iota(jnp.int32, (2 * NX * AR, 128), 0)
    lane2 = lax.broadcasted_iota(jnp.int32, (2 * NX * AR, 128), 1)
    x_of, b_of, u_of = (row // AR) % NX, (row % AR) // AB, row // (NX * AR)
    eye = lax.broadcasted_iota(jnp.int32, (HD, HD), 0) == lax.broadcasted_iota(jnp.int32, (HD, HD), 1)
    ones_vid = jnp.ones((2 * NX * VR, HD), BF16)

    def audio_pair(it, carry):
        z0, z1 = (z + 2 * it) % NZ, (z + 2 * it + 1) % NZ
        q = jnp.concatenate([aq[z0].reshape(NX * AR, HD), aq[z1].reshape(NX * AR, HD)], axis=0)
        zz = (z + 2 * it + u_of) % NZ
        block = ((c * NX + x_of) * NZ + zz) * 2 + b_of
        q = jnp.concatenate([q, jnp.where(lane2 == block, 1.0, 0.0).astype(BF16)], axis=1)
        key = jnp.concatenate([vk[...].reshape(2 * NX * VR, HD), kb[...].reshape(2 * NX * VR, HD)], axis=1)
        s = nt(q, key)
        top = jnp.max(s, axis=1, keepdims=True)
        p = jnp.exp2((s - top) * C2).astype(BF16)
        v = jnp.concatenate([vv[...].reshape(2 * NX * VR, HD), ones_vid], axis=1)
        o = jnp.dot(p, v, preferred_element_type=F32)
        part = (o[:, :HD] / o[:, HD:]).astype(BF16)
        level = top * C2 + jnp.log2(o[:, HD:])
        for u in range(2):
            d = 2 * it + u
            rows = slice(u * NX * AR, (u + 1) * NX * AR)
            flat = jnp.sum(jnp.where(eye, level[rows], 0.0), axis=0, keepdims=True)
            flat = jnp.broadcast_to(flat, (8, HD))

            def keep(d=d, rows=rows, flat=flat):
                po[d] = part[rows]
                pst[d] = flat
                slot = NZ - d
                to = dev(yh, x, (z + d) % NZ, yl, c)
                for t, (src, dst) in enumerate(((po, pr), (pst, prs))):
                    pltpu.make_async_remote_copy(
                        src_ref=src.at[d], dst_ref=dst.at[slot], send_sem=s_p.at[t, d], recv_sem=r_p.at[t, slot],
                        device_id=to, device_id_type=MESH,
                    ).start()

            if u:
                keep()
            else:

                @pl.when(it == 0)
                def _(rows=rows, flat=flat):
                    pr[0] = part[rows]
                    prs[0] = flat

                pl.when(it > 0)(keep)
        return carry

    lax.fori_loop(0, NZ // 2, audio_pair, 0)

    for copy in own_w:
        copy.wait()
    for t, ref in enumerate((wv, wa)):
        wait(ref.at[1 - c], r_w.at[t])
    for h in range(2 * NX):
        wait(va.at[h], r_vo.at[h])
    xv = jnp.concatenate(
        [
            jnp.concatenate([va[h, 1 - yl] for h in range(2 * NX)], axis=1),
            jnp.concatenate([va[h, yl] for h in range(2 * NX)], axis=1),
        ],
        axis=0,
    )
    n_chunks = ysend.shape[0]
    width = ysend.shape[2]

    def y_copy(n):
        return pltpu.make_async_remote_copy(
            src_ref=ysend.at[n], dst_ref=yrecv.at[n], send_sem=s_y.at[n], recv_sem=r_y.at[n],
            device_id=yl_peer, device_id_type=MESH,
        )

    def project(n, carry):
        at = pl.ds(pl.multiple_of(n * width, width), width)
        w = jnp.concatenate([wv[0, :, at], wv[1, :, at]], axis=0)
        y = jnp.dot(xv, w, preferred_element_type=F32)
        ysend[n] = y[: VB // 2].astype(BF16)
        yown[n] = y[VB // 2 :]
        y_copy(n).start()
        return carry

    lax.fori_loop(0, n_chunks, project, 0)

    for d in range(1, NZ):
        wait(pr.at[d], r_p.at[0, d])
        wait(prs.at[d], r_p.at[1, d])
    levels = jnp.concatenate([prs[d, 0:1, :] for d in range(NZ)], axis=0)
    share = jnp.exp2(levels - jnp.max(levels, axis=0, keepdims=True))
    share = share / jnp.sum(share, axis=0, keepdims=True)
    share = jnp.transpose(jnp.concatenate([share, jnp.zeros((HD - NZ, HD), F32)], axis=0))
    mixed = share[:, 0:1] * pr[0].astype(F32)
    for d in range(1, NZ):
        mixed = mixed + share[:, d : d + 1] * pr[d].astype(F32)
    mixed = mixed.reshape(NX, 2, 2, 8, HD)
    for k in range(2):
        ao[k] = mixed[:, :, k].reshape(NX, 16, HD).astype(BF16)
    for j in range(NX):
        for k in range(2):
            copy = pltpu.make_async_remote_copy(
                src_ref=ao.at[k, (x + j) % NX], dst_ref=aa.at[my_slot], send_sem=s_ao.at[j, k], recv_sem=r_ao.at[my_slot],
                device_id=dev(c, (x + j) % NX, z, yl, k), device_id_type=MESH,
            )
            if j:
                copy.start()
            else:
                to_self = is_self & (c == k)

                @pl.when(to_self)
                def _(k=k):
                    pltpu.make_async_copy(ao.at[k, x], aa.at[my_slot], r_ao.at[my_slot]).start()

                @pl.when(jnp.logical_not(to_self))
                def _(copy=copy):
                    copy.start()

    def finish(n, carry):
        y_copy(n).wait_recv()
        at = pl.ds(pl.multiple_of(n * width, width), width)
        ov[:, at] = (yown[n] + yrecv[n].astype(F32)).astype(BF16)
        return carry

    lax.fori_loop(0, n_chunks, finish, 0)

    for h in range(2 * NX):
        wait(aa.at[h], r_ao.at[h])
    xa = jnp.concatenate([aa[h] for h in range(2 * NX)], axis=1)
    for n in range(wa.shape[2] // 512):
        at = slice(n * 512, (n + 1) * 512)
        w = jnp.concatenate([wa[0, :, at], wa[1, :, at]], axis=0)
        asend[:, :, at] = jnp.dot(xa, w, preferred_element_type=F32).reshape(2, 8, 512)
    last = pltpu.make_async_remote_copy(
        src_ref=asend.at[1 - yl], dst_ref=arecv, send_sem=s_ya, recv_sem=r_ya, device_id=yl_peer, device_id_type=MESH
    )
    last.start()
    last.wait_recv()
    oa[...] = (asend[yl] + arecv[...]).astype(BF16)

    last.wait_send()
    for copy in other_w + vf + sent:
        copy.wait_send()

    def y_sent(n, carry):
        y_copy(n).wait_send()
        return carry

    lax.fori_loop(0, n_chunks, y_sent, 0)

    def f_sent(zz, carry):
        wait(ak.at[half, zz], s_f.at[0, zz])
        wait(av.at[half, zz], s_f.at[1, zz])
        return carry

    lax.fori_loop(0, NZ, f_sent, 0)
    for d in range(1, NZ):
        wait(po.at[d], s_p.at[0, d])
        wait(pst.at[d], s_p.at[1, d])

    def sent_exchange(j):
        for t in range(3):
            wait(aq.at[z, x], s_pa.at[t, j])
            wait(vq.at[x], s_pb.at[t, j])

    for j in range(1, NX):
        sent_exchange(j)

    @pl.when(jnp.logical_not(is_self))
    def _():
        sent_exchange(0)

    for j in range(NX):
        for k in range(2):

            def done(j=j, k=k):
                wait(va.at[my_slot], s_vo.at[j, k])
                wait(aa.at[my_slot], s_ao.at[j, k])

            if j:
                done()
            else:
                pl.when(jnp.logical_not(is_self & (c == k)))(done)


def shards(vq, vk, vv, aq, ak, av, ws, wv, wa):
    n_chunks = 8
    dv, da = wv.shape[1], wa.shape[1]
    dma = pltpu.SemaphoreType.DMA
    vmem = pltpu.VMEM
    scratch = [
        vmem((NX, VR, HD), BF16),
        vmem((2, NX, VR, HD), BF16),
        vmem((2, NX, VR, HD), BF16),
        vmem((NZ, NX, AR, HD), BF16),
        vmem((2 * NX * NZ * AR // AB, AB, HD), BF16),
        vmem((2 * NX * NZ * AR // AB, AB, HD), BF16),
        vmem((2,) + wv.shape, BF16),
        vmem((2,) + wa.shape, BF16),
        vmem((2, NX, VR, HD), BF16),
        vmem((NX, 2, 2, VB // 2, HD), BF16),
        vmem((2 * NX, 2, VB // 2, HD), BF16),
        vmem((NZ, NX * AR, HD), BF16),
        vmem((NZ, 8, HD), F32),
        vmem((NZ, NX * AR, HD), BF16),
        vmem((NZ, 8, HD), F32),
        vmem((2, NX, 16, HD), BF16),
        vmem((2 * NX, 16, HD), BF16),
        vmem((n_chunks, VB // 2, dv // n_chunks), BF16),
        vmem((n_chunks, VB // 2, dv // n_chunks), BF16),
        vmem((n_chunks, VB // 2, dv // n_chunks), F32),
        vmem((2, 8, da), F32),
        vmem((8, da), F32),
        dma((3, NX)), dma((3, NX)),
        dma((3, NX)), dma((3, NX)),
        dma((2, 3, NZ // 2)), dma((2, 3, NZ // 2)),
        dma((2, NZ)), dma((2, NZ)),
        dma((2,)), dma((2,)),
        dma((2,)), dma((2,)),
        dma((NX, 2)), dma((2 * NX,)),
        dma((2, NZ)), dma((2, NZ)),
        dma((NX, 2)), dma((2 * NX,)),
        dma((n_chunks,)), dma((n_chunks,)),
        dma, dma,
        dma((2,)),
    ]
    any_spec = pl.BlockSpec(memory_space=pl.ANY)
    return pl.pallas_call(
        kernel,
        out_shape=(
            jax.ShapeDtypeStruct((vq.shape[0] // 4, dv), BF16),
            jax.ShapeDtypeStruct((aq.shape[0] // 4, da), BF16),
        ),
        in_specs=[pl.BlockSpec(memory_space=pltpu.SMEM)] + [any_spec] * 8,
        out_specs=(pl.BlockSpec(memory_space=pltpu.VMEM), pl.BlockSpec(memory_space=pltpu.VMEM)),
        scratch_shapes=scratch,
        compiler_params=pltpu.CompilerParams(
            collective_id=0, has_side_effects=True, vmem_limit_bytes=48 * 1024 * 1024
        ),
        cost_estimate=pl.CostEstimate(flops=3_000_000_000, bytes_accessed=16_000_000, transcendentals=4_000_000),
    )(ws, vq, vk, vv, aq, ak, av, wv, wa)


def solution(mesh):
    part = P("seq", "head")
    in_specs = (part, part, part, part, part, part, P(), P("head", None), P("head", None))
    out_specs = (P(("seq", "head"), None), P(("seq", "head"), None))
    return jax.shard_map(shards, mesh=mesh, in_specs=in_specs, out_specs=out_specs, check_vma=False)
```

```python
import math

import jax
import jax.numpy as jnp
from jax import lax
from jax.experimental import pallas as pl
from jax.experimental.pallas import tpu as pltpu
from jax.sharding import PartitionSpec as P

HD = 128
VB = 128
AB = 16
WIN = 80
NX, NZ = 4, 8
VR = 256
AR = 32
NEG = -1e30
C2 = math.log2(math.e) / math.sqrt(HD)
MESH = pl.DeviceIdType.MESH
F32, BF16 = jnp.float32, jnp.bfloat16


def dev(yh, x, z, yl, c):
    return ((yh * NX + x) * NZ + z, yl * 2 + c)


def nt(a, b):
    return lax.dot_general(a, b, (((1,), (1,)), ((), ())), preferred_element_type=F32)


def kernel(
    ws, vq_in, vk_in, vv_in, aq_in, ak_in, av_in, wv_in, wa_in, ov, oa,
    vq, vk, vv, aq, ak_flat, av_flat, wv, wa, kb, vo, va, po, pst, pr, prs, ao, aa, ysend, yrecv, yown, asend, arecv,
    s_pa, r_pa, s_pb, r_pb, s_z, r_z, s_f, r_f, s_vf, r_vf, s_w, r_w, s_vo, r_vo, s_p, r_p, s_ao, r_ao, s_y, r_y, s_ya, r_ya, l_w,
):
    seq, head = lax.axis_index("seq"), lax.axis_index("head")
    yh, x, z = seq // (NX * NZ), (seq // NZ) % NX, seq % NZ
    yl, c = head // 2, head % 2
    ak, av = (ref.reshape(2 * NX, NZ, AR, HD) for ref in (ak_flat, av_flat))
    is_self = yh == c
    core_peer = dev(yh, x, z, yl, 1 - c)
    yl_peer = dev(yh, x, z, 1 - yl, c)
    cross_peer = dev(1 - yh, x, z, 1 - yl, c)

    def peer(j):
        return dev(c, (x + j) % NX, z, yl, yh)

    drains = []

    def wait(ref, sem):
        pltpu.make_async_copy(ref, ref, sem).wait()

    own_w = [
        pltpu.make_async_copy(wv_in, wv.at[c], l_w.at[0]),
        pltpu.make_async_copy(wa_in, wa.at[c], l_w.at[1]),
    ]
    for copy in own_w:
        copy.start()

    barrier = pltpu.get_barrier_semaphore()

    def greet(device):
        pl.semaphore_signal(barrier, inc=1, device_id=device, device_id_type=MESH)

    group = [(p, j, q) for p in range(2) for j in range(NX) for q in range(2) if p or j or q]
    for p, j, q in group:
        greet(dev((yh + p) % 2, (x + j) % NX, z, yl, (c + q) % 2))
    for d in range(1, NZ):
        greet(dev(yh, x, (z + d) % NZ, yl, c))
    greet(yl_peer)
    greet(cross_peer)
    pl.semaphore_wait(barrier, len(group) + NZ + 1)

    def exchange(src, dst, send, recv, j):
        remote = pltpu.make_async_remote_copy(
            src_ref=src, dst_ref=dst, send_sem=send, recv_sem=recv, device_id=peer(j), device_id_type=MESH
        )
        if j:
            remote.start()
            return

        @pl.when(is_self)
        def _():
            pltpu.make_async_copy(src, dst, recv).start()

        @pl.when(jnp.logical_not(is_self))
        def _():
            remote.start()

    def cols(j):
        return pl.ds(pl.multiple_of(((x + j) % NX) * HD, HD), HD)

    here = yh * NX + x
    for j in range(NX):
        exchange(aq_in.at[:, cols(j)], aq.at[z, x], s_pa.at[0, j], r_pa.at[0, x], j)
        exchange(ak_in.at[:, cols(j)], ak.at[here, z], s_pa.at[1, j], r_pa.at[1, x], j)
        exchange(av_in.at[:, cols(j)], av.at[here, z], s_pa.at[2, j], r_pa.at[2, x], j)
    for t, (src, dst) in enumerate(((vk_in, vk.at[yh]), (vv_in, vv.at[yh]), (vq_in, vq))):
        for j in range(NX):
            exchange(src.at[:, cols(j)], dst.at[x], s_pb.at[t, j], r_pb.at[t, x], j)

    def exchange_sent():
        def one(j):
            for t in range(3):
                wait(aq.at[z, x], s_pa.at[t, j])
                wait(vq.at[x], s_pb.at[t, j])

        for j in range(1, NX):
            one(j)
        pl.when(jnp.logical_not(is_self))(lambda: one(0))

    drains.append(exchange_sent)

    other_w = [
        pltpu.make_async_remote_copy(
            src_ref=src, dst_ref=dst.at[c], send_sem=s_w.at[t], recv_sem=r_w.at[t],
            device_id=core_peer, device_id_type=MESH,
        )
        for t, (src, dst) in enumerate(((wv_in, wv), (wa_in, wa)))
    ]
    for copy in other_w:
        copy.start()

    drains.extend(copy.wait_send for copy in other_w)

    lane = lax.broadcasted_iota(jnp.int32, (VB, 128), 1)
    for a in range(2):
        for xs in range(NX):
            for i in range(2):
                start = ws[((a * NX + xs) * NZ + z) * 2 + i]
                inside = (lane >= start) & (lane < start + WIN)
                kb[a, xs, pl.ds(i * VB, VB), :] = jnp.where(inside, 0.0, NEG).astype(BF16)

    for xs in range(NX):
        wait(aq.at[z, xs], r_pa.at[0, xs])
        wait(ak.at[c * NX + xs, z], r_pa.at[1, xs])
        wait(av.at[c * NX + xs, z], r_pa.at[2, xs])

    half = pl.ds(c * NX, NX)
    other_half = pl.ds((1 - c) * NX, NX)

    def chunk(t, zz):
        return aq.at[zz] if t == 0 else (ak, av)[t - 1].at[half, zz]

    def forward(t, zz):
        pltpu.make_async_remote_copy(
            src_ref=chunk(t, zz), dst_ref=chunk(t, zz), send_sem=s_f.at[t - 1, zz], recv_sem=r_f.at[t - 1, zz],
            device_id=core_peer, device_id_type=MESH,
        ).start()

    vf = []

    def share_video():
        for t, ref in enumerate((vk, vv)):
            for xs in range(NX):
                wait(ref.at[c, xs], r_pb.at[t, xs])
            copy = pltpu.make_async_remote_copy(
                src_ref=ref.at[c], dst_ref=ref.at[c], send_sem=s_vf.at[t], recv_sem=r_vf.at[t],
                device_id=core_peer, device_id_type=MESH,
            )
            copy.start()
            vf.append(copy)

    def hop_copy(way, t, k):
        zz = (z - k + 1 + NZ) % NZ if way == 0 else (z + k - 1) % NZ
        to = (z + 1) % NZ if way == 0 else (z + NZ - 1) % NZ
        return pltpu.make_async_remote_copy(
            src_ref=chunk(t, zz), dst_ref=chunk(t, zz), send_sem=s_z.at[way, t, k - 1], recv_sem=r_z.at[way, t, k - 1],
            device_id=dev(yh, x, to, yl, c), device_id_type=MESH,
        )

    def arrived(way, t, k):
        zz = (z - k + NZ) % NZ if way == 0 else (z + k) % NZ
        wait(chunk(t, zz), r_z.at[way, t, k - 1])
        if t:
            forward(t, zz)

    sent = []
    last_hops = [(0, 1), (1, 2), (0, 0)]

    def hops(k):
        return last_hops if k == NZ // 2 else [(way, t) for t in (1, 2, 0) for way in range(2)]

    for k in range(1, NZ // 2 + 1):
        if k == NZ // 2:
            share_video()
        for t in (1, 2, 0):
            for way in range(2):
                if k == 1:
                    if t and way == 0:
                        forward(t, z)
                else:
                    arrived(way, t, k - 1)
                if (way, t) in hops(k):
                    sent.append(hop_copy(way, t, k))
                    sent[-1].start()

    def gather_end():
        for way, t in last_hops:
            arrived(way, t, NZ // 2)

    def gather_sent():
        for copy in sent:
            copy.wait_send()

        def one(zz, carry):
            wait(ak.at[half, zz], s_f.at[0, zz])
            wait(av.at[half, zz], s_f.at[1, zz])
            return carry

        lax.fori_loop(0, NZ, one, 0)

    drains.append(gather_sent)

    drains.extend(copy.wait_send for copy in vf)

    for t, ref in enumerate((vk, vv)):
        wait(ref.at[1 - c], r_vf.at[t])
    row = lax.broadcasted_iota(jnp.int32, (2 * NX * AR, 128), 0)
    lane2 = lax.broadcasted_iota(jnp.int32, (2 * NX * AR, 128), 1)
    x_of, b_of, u_of = (row // AR) % NX, (row % AR) // AB, row // (NX * AR)
    eye = lax.broadcasted_iota(jnp.int32, (HD, HD), 0) == lax.broadcasted_iota(jnp.int32, (HD, HD), 1)
    ones_vid = jnp.ones((2 * NX * VR, HD), BF16)

    def audio_pair(it, carry):
        pl.when(it == NZ // 4)(gather_end)
        z0, z1 = (z + 2 * it) % NZ, (z + 2 * it + 1) % NZ
        q = jnp.concatenate([aq[z0].reshape(NX * AR, HD), aq[z1].reshape(NX * AR, HD)], axis=0)
        zz = (z + 2 * it + u_of) % NZ
        block = ((c * NX + x_of) * NZ + zz) * 2 + b_of
        q = jnp.concatenate([q, jnp.where(lane2 == block, 1.0, 0.0).astype(BF16)], axis=1)
        key = jnp.concatenate([vk[...].reshape(2 * NX * VR, HD), kb[...].reshape(2 * NX * VR, HD)], axis=1)
        s = nt(q, key)
        top = jnp.max(s, axis=1, keepdims=True)
        p = jnp.exp2((s - top) * C2).astype(BF16)
        v = jnp.concatenate([vv[...].reshape(2 * NX * VR, HD), ones_vid], axis=1)
        o = jnp.dot(p, v, preferred_element_type=F32)
        part = (o[:, :HD] / o[:, HD:]).astype(BF16)
        level = top * C2 + jnp.log2(o[:, HD:])
        for u in range(2):
            d = 2 * it + u
            rows = slice(u * NX * AR, (u + 1) * NX * AR)
            flat = jnp.sum(jnp.where(eye, level[rows], 0.0), axis=0, keepdims=True)
            flat = jnp.broadcast_to(flat, (8, HD))

            def keep(d=d, rows=rows, flat=flat):
                po[d] = part[rows]
                pst[d] = flat
                slot = NZ - d
                to = dev(yh, x, (z + d) % NZ, yl, c)
                for t, (src, dst) in enumerate(((po, pr), (pst, prs))):
                    pltpu.make_async_remote_copy(
                        src_ref=src.at[d], dst_ref=dst.at[slot], send_sem=s_p.at[t, d], recv_sem=r_p.at[t, slot],
                        device_id=to, device_id_type=MESH,
                    ).start()

            if u:
                keep()
            else:

                @pl.when(it == 0)
                def _(rows=rows, flat=flat):
                    pr[0] = part[rows]
                    prs[0] = flat

                pl.when(it > 0)(keep)
        return carry

    lax.fori_loop(0, NZ // 2, audio_pair, 0)

    def parts_sent():
        for d in range(1, NZ):
            wait(po.at[d], s_p.at[0, d])
            wait(pst.at[d], s_p.at[1, d])

    drains.append(parts_sent)
    for xs in range(NX):
        wait(vq.at[xs], r_pb.at[2, xs])

    def late(zz, carry):
        wait(ak.at[other_half, zz], r_f.at[0, zz])
        wait(av.at[other_half, zz], r_f.at[1, zz])
        return carry

    lax.fori_loop(0, NZ, late, 0)

    ones_win = jnp.ones((WIN * AB, HD), BF16)

    my_slot = yh * NX + x

    def video_rows(n, carry):
        j = (n + 2) % NX
        xs = (x + j) % NX
        for i in range(2):
            start = ws[((c * NX + xs) * NZ + z) * 2 + i]
            blocks = pl.ds(start, WIN)
            s = nt(vq[xs, pl.ds(i * VB, VB), :], ak_flat[blocks].reshape(WIN * AB, HD))
            top = jnp.max(s, axis=1, keepdims=True)
            p = jnp.exp2((s - top) * C2).astype(BF16)
            v = jnp.concatenate([av_flat[blocks].reshape(WIN * AB, HD), ones_win], axis=1)
            o = jnp.dot(p, v, preferred_element_type=F32)
            o = (o[:, :HD] / o[:, HD:]).astype(BF16)
            at = pl.ds(pl.multiple_of(jnp.where(yl == i, VB // 2, 0), VB // 2), VB // 2)
            for k in range(2):
                vo[xs, k, at, :] = o[k * VB // 2 : (k + 1) * VB // 2]
        for k in range(2):
            for m, (to, rows) in enumerate(((c, pl.ds(VB // 4, VB * 3 // 4)), (1 - c, pl.ds(0, VB // 4)))):
                src, dst, recv = vo.at[xs, k, rows], va.at[my_slot, rows], r_vo.at[m, my_slot]
                to_self = (j == 0) & (yh == to) & (c == k)

                @pl.when(to_self)
                def _(src=src, dst=dst, recv=recv):
                    pltpu.make_async_copy(src, dst, recv).start()

                @pl.when(jnp.logical_not(to_self))
                def _(src=src, dst=dst, recv=recv, to=to, k=k, m=m):
                    pltpu.make_async_remote_copy(
                        src_ref=src, dst_ref=dst, send_sem=s_vo.at[m, j, k], recv_sem=recv,
                        device_id=dev(to, xs, z, yl, k), device_id_type=MESH,
                    ).start()

        return carry

    lax.fori_loop(0, NX, video_rows, 0)

    def rows_sent(src, sems, to):
        for j in range(NX):
            for k in range(2):
                if j:
                    wait(src, sems.at[j, k])
                else:
                    pl.when(jnp.logical_not((yh == to) & (c == k)))(lambda k=k: wait(src, sems.at[0, k]))

    drains.append(lambda: rows_sent(va.at[my_slot, pl.ds(VB // 4, VB * 3 // 4)], s_vo.at[0], c))
    drains.append(lambda: rows_sent(va.at[my_slot, pl.ds(0, VB // 4)], s_vo.at[1], 1 - c))

    for copy in own_w:
        copy.wait()
    for t, ref in enumerate((wv, wa)):
        wait(ref.at[1 - c], r_w.at[t])
    for h in range(2 * NX):
        wait(va.at[h, pl.ds(VB // 4, VB * 3 // 4)], r_vo.at[0, h])
        wait(va.at[h, pl.ds(0, VB // 4)], r_vo.at[1, h])
    xv = jnp.concatenate([va[h] for h in range(2 * NX)], axis=1)
    n_chunks = ysend.shape[0]
    width = ysend.shape[2]

    def y_copy(n, m):
        rows = pl.ds(m * VB // 4, VB // 4)
        return pltpu.make_async_remote_copy(
            src_ref=ysend.at[n, rows], dst_ref=yrecv.at[n, rows], send_sem=s_y.at[m, n], recv_sem=r_y.at[m, n],
            device_id=(cross_peer, yl_peer)[m], device_id_type=MESH,
        )

    def project(n, carry):
        at = pl.ds(pl.multiple_of(n * width, width), width)
        w = jnp.concatenate([wv[0, :, at], wv[1, :, at]], axis=0)
        y = jnp.dot(xv, w, preferred_element_type=F32)
        ysend[n] = y[: VB // 2].astype(BF16)
        yown[n] = y[VB // 2 :]
        for m in range(2):
            y_copy(n, m).start()
        return carry

    lax.fori_loop(0, n_chunks, project, 0)

    def y_sent():
        def one(n, carry):
            for m in range(2):
                y_copy(n, m).wait_send()
            return carry

        lax.fori_loop(0, n_chunks, one, 0)

    drains.append(y_sent)

    for d in range(1, NZ):
        wait(pr.at[d], r_p.at[0, d])
        wait(prs.at[d], r_p.at[1, d])
    levels = jnp.concatenate([prs[d, 0:1, :] for d in range(NZ)], axis=0)
    share = jnp.exp2(levels - jnp.max(levels, axis=0, keepdims=True))
    share = share / jnp.sum(share, axis=0, keepdims=True)
    share = jnp.transpose(jnp.concatenate([share, jnp.zeros((HD - NZ, HD), F32)], axis=0))
    mixed = share[:, 0:1] * pr[0].astype(F32)
    for d in range(1, NZ):
        mixed = mixed + share[:, d : d + 1] * pr[d].astype(F32)
    mixed = mixed.reshape(NX, 2, 2, 8, HD)
    for k in range(2):
        ao[k] = mixed[:, :, k].reshape(NX, 16, HD).astype(BF16)
    for j in range(NX):
        for k in range(2):
            copy = pltpu.make_async_remote_copy(
                src_ref=ao.at[k, (x + j) % NX], dst_ref=aa.at[my_slot], send_sem=s_ao.at[j, k], recv_sem=r_ao.at[my_slot],
                device_id=dev(c, (x + j) % NX, z, yl, k), device_id_type=MESH,
            )
            if j:
                copy.start()
            else:
                to_self = is_self & (c == k)

                @pl.when(to_self)
                def _(k=k):
                    pltpu.make_async_copy(ao.at[k, x], aa.at[my_slot], r_ao.at[my_slot]).start()

                @pl.when(jnp.logical_not(to_self))
                def _(copy=copy):
                    copy.start()

    drains.append(lambda: rows_sent(aa.at[my_slot], s_ao, c))

    def finish(n, carry):
        for m in range(2):
            y_copy(n, m).wait_recv()
        at = pl.ds(pl.multiple_of(n * width, width), width)
        ov[:, at] = (yown[n] + yrecv[n].astype(F32)).astype(BF16)
        return carry

    lax.fori_loop(0, n_chunks, finish, 0)

    for h in range(2 * NX):
        wait(aa.at[h], r_ao.at[h])
    xa = jnp.concatenate([aa[h] for h in range(2 * NX)], axis=1)
    for n in range(wa.shape[2] // 512):
        at = slice(n * 512, (n + 1) * 512)
        w = jnp.concatenate([wa[0, :, at], wa[1, :, at]], axis=0)
        asend[:, :, at] = jnp.dot(xa, w, preferred_element_type=F32).reshape(2, 8, 512)
    last = pltpu.make_async_remote_copy(
        src_ref=asend.at[1 - yl], dst_ref=arecv, send_sem=s_ya, recv_sem=r_ya, device_id=yl_peer, device_id_type=MESH
    )
    last.start()
    drains.append(last.wait_send)
    last.wait_recv()
    oa[...] = (asend[yl] + arecv[...]).astype(BF16)

    for drain in drains:
        drain()


def shards(vq, vk, vv, aq, ak, av, ws, wv, wa):
    n_chunks = 8
    dv, da = wv.shape[1], wa.shape[1]
    dma = pltpu.SemaphoreType.DMA
    vmem = pltpu.VMEM
    scratch = [
        vmem((NX, VR, HD), BF16),
        vmem((2, NX, VR, HD), BF16),
        vmem((2, NX, VR, HD), BF16),
        vmem((NZ, NX, AR, HD), BF16),
        vmem((2 * NX * NZ * AR // AB, AB, HD), BF16),
        vmem((2 * NX * NZ * AR // AB, AB, HD), BF16),
        vmem((2,) + wv.shape, BF16),
        vmem((2,) + wa.shape, BF16),
        vmem((2, NX, VR, HD), BF16),
        vmem((NX, 2, VB, HD), BF16),
        vmem((2 * NX, VB, HD), BF16),
        vmem((NZ, NX * AR, HD), BF16),
        vmem((NZ, 8, HD), F32),
        vmem((NZ, NX * AR, HD), BF16),
        vmem((NZ, 8, HD), F32),
        vmem((2, NX, 16, HD), BF16),
        vmem((2 * NX, 16, HD), BF16),
        vmem((n_chunks, VB // 2, dv // n_chunks), BF16),
        vmem((n_chunks, VB // 2, dv // n_chunks), BF16),
        vmem((n_chunks, VB // 2, dv // n_chunks), F32),
        vmem((2, 8, da), F32),
        vmem((8, da), F32),
        dma((3, NX)), dma((3, NX)),
        dma((3, NX)), dma((3, NX)),
        dma((2, 3, NZ // 2)), dma((2, 3, NZ // 2)),
        dma((2, NZ)), dma((2, NZ)),
        dma((2,)), dma((2,)),
        dma((2,)), dma((2,)),
        dma((2, NX, 2)), dma((2, 2 * NX)),
        dma((2, NZ)), dma((2, NZ)),
        dma((NX, 2)), dma((2 * NX,)),
        dma((2, n_chunks)), dma((2, n_chunks)),
        dma, dma,
        dma((2,)),
    ]
    any_spec = pl.BlockSpec(memory_space=pl.ANY)
    return pl.pallas_call(
        kernel,
        out_shape=(
            jax.ShapeDtypeStruct((vq.shape[0] // 4, dv), BF16),
            jax.ShapeDtypeStruct((aq.shape[0] // 4, da), BF16),
        ),
        in_specs=[pl.BlockSpec(memory_space=pltpu.SMEM)] + [any_spec] * 8,
        out_specs=(pl.BlockSpec(memory_space=pltpu.VMEM), pl.BlockSpec(memory_space=pltpu.VMEM)),
        scratch_shapes=scratch,
        compiler_params=pltpu.CompilerParams(
            collective_id=0, has_side_effects=True, vmem_limit_bytes=60 * 1024 * 1024
        ),
        cost_estimate=pl.CostEstimate(flops=3_000_000_000, bytes_accessed=16_000_000, transcendentals=4_000_000),
    )(ws, vq, vk, vv, aq, ak, av, wv, wa)


def solution(mesh):
    part = P("seq", "head")
    in_specs = (part, part, part, part, part, part, P(), P("head", None), P("head", None))
    out_specs = (P(("seq", "head"), None), P(("seq", "head"), None))
    return jax.shard_map(shards, mesh=mesh, in_specs=in_specs, out_specs=out_specs, check_vma=False)
```

```python
import math

import jax
import jax.numpy as jnp
from jax import lax
from jax.experimental import pallas as pl
from jax.experimental.pallas import tpu as pltpu
from jax.sharding import PartitionSpec as P

HD = 128
VB = 128
AB = 16
WIN = 80
NX, NZ = 4, 8
VR = 256
AR = 32
NEG = -1e30
C2 = math.log2(math.e) / math.sqrt(HD)
MESH = pl.DeviceIdType.MESH
F32, BF16 = jnp.float32, jnp.bfloat16


def dev(yh, x, z, yl, c):
    return ((yh * NX + x) * NZ + z, yl * 2 + c)


def nt(a, b):
    return lax.dot_general(a, b, (((1,), (1,)), ((), ())), preferred_element_type=F32)


def kernel(
    ws, vq_in, vk_in, vv_in, aq_in, ak_in, av_in, wv_in, wa_in, ov, oa,
    vq, vk, vv, aq, ak_flat, av_flat, wv, wa, kb, vo, va, po, pst, pr, prs, ao, aa, ysend, yrecv, yown, asend, arecv,
    s_pa, r_pa, s_pb, r_pb, s_z, r_z, s_f, r_f, s_vf, r_vf, s_w, r_w, s_vo, r_vo, s_p, r_p, s_ao, r_ao, s_y, r_y, s_ya, r_ya, l_w,
):
    seq, head = lax.axis_index("seq"), lax.axis_index("head")
    yh, x, z = seq // (NX * NZ), (seq // NZ) % NX, seq % NZ
    yl, c = head // 2, head % 2
    ak, av = (ref.reshape(2 * NX, NZ, AR, HD) for ref in (ak_flat, av_flat))
    is_self = yh == c
    core_peer = dev(yh, x, z, yl, 1 - c)
    yl_peer = dev(yh, x, z, 1 - yl, c)
    cross_peer = dev(1 - yh, x, z, 1 - yl, c)

    def peer(j):
        return dev(c, (x + j) % NX, z, yl, yh)

    drains = []

    def wait(ref, sem):
        pltpu.make_async_copy(ref, ref, sem).wait()

    own_w = [
        pltpu.make_async_copy(wv_in, wv.at[c], l_w.at[0]),
        pltpu.make_async_copy(wa_in, wa.at[c], l_w.at[1]),
    ]
    for copy in own_w:
        copy.start()

    barrier = pltpu.get_barrier_semaphore()

    def greet(device):
        pl.semaphore_signal(barrier, inc=1, device_id=device, device_id_type=MESH)

    group = [(p, j, q) for p in range(2) for j in range(NX) for q in range(2) if p or j or q]
    for p, j, q in group:
        greet(dev((yh + p) % 2, (x + j) % NX, z, yl, (c + q) % 2))
    for d in range(1, NZ):
        greet(dev(yh, x, (z + d) % NZ, yl, c))
    greet(yl_peer)
    greet(cross_peer)
    pl.semaphore_wait(barrier, len(group) + NZ + 1)

    def exchange(src, dst, send, recv, j):
        remote = pltpu.make_async_remote_copy(
            src_ref=src, dst_ref=dst, send_sem=send, recv_sem=recv, device_id=peer(j), device_id_type=MESH
        )
        if j:
            remote.start()
            return

        @pl.when(is_self)
        def _():
            pltpu.make_async_copy(src, dst, recv).start()

        @pl.when(jnp.logical_not(is_self))
        def _():
            remote.start()

    def cols(j):
        return pl.ds(pl.multiple_of(((x + j) % NX) * HD, HD), HD)

    here = yh * NX + x
    for j in range(NX):
        exchange(aq_in.at[:, cols(j)], aq.at[z, x], s_pa.at[0, j], r_pa.at[0, x], j)
        exchange(ak_in.at[:, cols(j)], ak.at[here, z], s_pa.at[1, j], r_pa.at[1, x], j)
        exchange(av_in.at[:, cols(j)], av.at[here, z], s_pa.at[2, j], r_pa.at[2, x], j)
    def audio_sent(j):
        for t in range(3):
            wait(aq.at[z, x], s_pa.at[t, j])

    for j in range(1, NX):
        audio_sent(j)
    pl.when(jnp.logical_not(is_self))(lambda: audio_sent(0))
    for t, (src, dst) in enumerate(((vk_in, vk.at[yh]), (vv_in, vv.at[yh]), (vq_in, vq))):
        for j in range(NX):
            exchange(src.at[:, cols(j)], dst.at[x], s_pb.at[t, j], r_pb.at[t, x], j)

    def exchange_sent():
        def one(j):
            for t in range(3):
                wait(vq.at[x], s_pb.at[t, j])

        for j in range(1, NX):
            one(j)
        pl.when(jnp.logical_not(is_self))(lambda: one(0))

    drains.append(exchange_sent)

    lane = lax.broadcasted_iota(jnp.int32, (VB, 128), 1)
    for a in range(2):
        for xs in range(NX):
            for i in range(2):
                start = ws[((a * NX + xs) * NZ + z) * 2 + i]
                inside = (lane >= start) & (lane < start + WIN)
                kb[a, xs, pl.ds(i * VB, VB), :] = jnp.where(inside, 0.0, NEG).astype(BF16)

    for xs in range(NX):
        wait(aq.at[z, xs], r_pa.at[0, xs])
        wait(ak.at[c * NX + xs, z], r_pa.at[1, xs])
        wait(av.at[c * NX + xs, z], r_pa.at[2, xs])

    half = pl.ds(c * NX, NX)
    other_half = pl.ds((1 - c) * NX, NX)

    def chunk(t, zz):
        return aq.at[zz] if t == 0 else (ak, av)[t - 1].at[half, zz]

    def forward(t, zz):
        pltpu.make_async_remote_copy(
            src_ref=chunk(t, zz), dst_ref=chunk(t, zz), send_sem=s_f.at[t - 1, zz], recv_sem=r_f.at[t - 1, zz],
            device_id=core_peer, device_id_type=MESH,
        ).start()

    vf = []

    def share_video():
        for t, ref in enumerate((vk, vv)):
            for xs in range(NX):
                wait(ref.at[c, xs], r_pb.at[t, xs])
            copy = pltpu.make_async_remote_copy(
                src_ref=ref.at[c], dst_ref=ref.at[c], send_sem=s_vf.at[t], recv_sem=r_vf.at[t],
                device_id=core_peer, device_id_type=MESH,
            )
            copy.start()
            vf.append(copy)

    def hop_copy(way, t, k):
        zz = (z - k + 1 + NZ) % NZ if way == 0 else (z + k - 1) % NZ
        to = (z + 1) % NZ if way == 0 else (z + NZ - 1) % NZ
        return pltpu.make_async_remote_copy(
            src_ref=chunk(t, zz), dst_ref=chunk(t, zz), send_sem=s_z.at[way, t, k - 1], recv_sem=r_z.at[way, t, k - 1],
            device_id=dev(yh, x, to, yl, c), device_id_type=MESH,
        )

    def arrived(way, t, k):
        zz = (z - k + NZ) % NZ if way == 0 else (z + k) % NZ
        wait(chunk(t, zz), r_z.at[way, t, k - 1])
        if t:
            forward(t, zz)

    last_hops = [(0, 1), (1, 2), (0, 0)]

    def hops(k):
        return last_hops if k == NZ // 2 else [(way, t) for t in (1, 2, 0) for way in range(2)]

    def hop(k):
        for t in (1, 2, 0):
            for way in range(2):
                if k > 1:
                    arrived(way, t, k - 1)
                elif t and way == 0:
                    forward(t, z)
                if (way, t) in hops(k):
                    hop_copy(way, t, k).start()

    for k in range(1, NZ // 2):
        hop(k)
    share_video()

    def gather_end():
        for way, t in last_hops:
            arrived(way, t, NZ // 2)

    def gather_sent():
        for k in range(1, NZ // 2 + 1):
            for way, t in hops(k):
                hop_copy(way, t, k).wait_send()

        def one(zz, carry):
            wait(ak.at[half, zz], s_f.at[0, zz])
            wait(av.at[half, zz], s_f.at[1, zz])
            return carry

        lax.fori_loop(0, NZ, one, 0)

    drains.append(gather_sent)

    drains.extend(copy.wait_send for copy in vf)

    other_w = [
        pltpu.make_async_remote_copy(
            src_ref=src, dst_ref=dst.at[c], send_sem=s_w.at[t], recv_sem=r_w.at[t],
            device_id=core_peer, device_id_type=MESH,
        )
        for t, (src, dst) in enumerate(((wv_in, wv), (wa_in, wa)))
    ]
    for copy in other_w:
        copy.start()

    drains.extend(copy.wait_send for copy in other_w)

    for t, ref in enumerate((vk, vv)):
        wait(ref.at[1 - c], r_vf.at[t])
    row = lax.broadcasted_iota(jnp.int32, (2 * NX * AR, 128), 0)
    lane2 = lax.broadcasted_iota(jnp.int32, (2 * NX * AR, 128), 1)
    x_of, b_of, u_of = (row // AR) % NX, (row % AR) // AB, row // (NX * AR)
    eye = lax.broadcasted_iota(jnp.int32, (HD, HD), 0) == lax.broadcasted_iota(jnp.int32, (HD, HD), 1)
    ones_vid = jnp.ones((2 * NX * VR, HD), BF16)

    def audio_pair(n, carry):
        pl.when(n == 1)(lambda: hop(NZ // 2))
        pl.when(n == NZ // 2 - 1)(gather_end)
        d0 = (n + 1) % (NZ // 2)
        d1 = jnp.where(d0 == 0, NZ // 2, NZ - d0)
        z0, z1 = (z + d0) % NZ, (z + d1) % NZ
        q = jnp.concatenate([aq[z0].reshape(NX * AR, HD), aq[z1].reshape(NX * AR, HD)], axis=0)
        zz = jnp.where(u_of == 0, z0, z1)
        block = ((c * NX + x_of) * NZ + zz) * 2 + b_of
        q = jnp.concatenate([q, jnp.where(lane2 == block, 1.0, 0.0).astype(BF16)], axis=1)
        key = jnp.concatenate([vk[...].reshape(2 * NX * VR, HD), kb[...].reshape(2 * NX * VR, HD)], axis=1)
        s = nt(q, key)
        top = jnp.max(s, axis=1, keepdims=True)
        p = jnp.exp2((s - top) * C2).astype(BF16)
        v = jnp.concatenate([vv[...].reshape(2 * NX * VR, HD), ones_vid], axis=1)
        o = jnp.dot(p, v, preferred_element_type=F32)
        part = (o[:, :HD] / o[:, HD:]).astype(BF16)
        level = top * C2 + jnp.log2(o[:, HD:])
        for u in range(2):
            d = d1 if u else d0
            rows = slice(u * NX * AR, (u + 1) * NX * AR)
            flat = jnp.sum(jnp.where(eye, level[rows], 0.0), axis=0, keepdims=True)
            flat = jnp.broadcast_to(flat, (8, HD))

            def keep(d=d, rows=rows, flat=flat):
                po[d] = part[rows]
                pst[d] = flat
                slot = NZ - d
                to = dev(yh, x, (z + d) % NZ, yl, c)
                for t, (src, dst) in enumerate(((po, pr), (pst, prs))):
                    pltpu.make_async_remote_copy(
                        src_ref=src.at[d], dst_ref=dst.at[slot], send_sem=s_p.at[t, d], recv_sem=r_p.at[t, slot],
                        device_id=to, device_id_type=MESH,
                    ).start()

            if u:
                keep()
            else:

                @pl.when(d == 0)
                def _(rows=rows, flat=flat):
                    pr[0] = part[rows]
                    prs[0] = flat

                pl.when(d > 0)(keep)
        return carry

    lax.fori_loop(0, NZ // 2, audio_pair, 0)

    def parts_sent():
        for d in range(1, NZ):
            wait(po.at[d], s_p.at[0, d])
            wait(pst.at[d], s_p.at[1, d])

    drains.append(parts_sent)
    for xs in range(NX):
        wait(vq.at[xs], r_pb.at[2, xs])

    def late(zz, carry):
        wait(ak.at[other_half, zz], r_f.at[0, zz])
        wait(av.at[other_half, zz], r_f.at[1, zz])
        return carry

    lax.fori_loop(0, NZ, late, 0)

    ones_win = jnp.ones((WIN * AB, HD), BF16)

    my_slot = yh * NX + x

    def video_rows(n, carry):
        j = (n + 2) % NX
        xs = (x + j) % NX
        for i in range(2):
            start = ws[((c * NX + xs) * NZ + z) * 2 + i]
            blocks = pl.ds(start, WIN)
            s = nt(vq[xs, pl.ds(i * VB, VB), :], ak_flat[blocks].reshape(WIN * AB, HD))
            top = jnp.max(s, axis=1, keepdims=True)
            p = jnp.exp2((s - top) * C2).astype(BF16)
            v = jnp.concatenate([av_flat[blocks].reshape(WIN * AB, HD), ones_win], axis=1)
            o = jnp.dot(p, v, preferred_element_type=F32)
            o = (o[:, :HD] / o[:, HD:]).astype(BF16)
            at = pl.ds(pl.multiple_of(jnp.where(yl == i, VB // 2, 0), VB // 2), VB // 2)
            for k in range(2):
                vo[xs, k, at, :] = o[k * VB // 2 : (k + 1) * VB // 2]
        for k in range(2):
            for m, (to, rows) in enumerate(((c, pl.ds(VB // 4, VB * 3 // 4)), (1 - c, pl.ds(0, VB // 4)))):
                src, dst, recv = vo.at[xs, k, rows], va.at[my_slot, rows], r_vo.at[m, my_slot]
                to_self = (j == 0) & (yh == to) & (c == k)

                @pl.when(to_self)
                def _(src=src, dst=dst, recv=recv):
                    pltpu.make_async_copy(src, dst, recv).start()

                @pl.when(jnp.logical_not(to_self))
                def _(src=src, dst=dst, recv=recv, to=to, k=k, m=m):
                    pltpu.make_async_remote_copy(
                        src_ref=src, dst_ref=dst, send_sem=s_vo.at[m, j, k], recv_sem=recv,
                        device_id=dev(to, xs, z, yl, k), device_id_type=MESH,
                    ).start()

        return carry

    lax.fori_loop(0, NX, video_rows, 0)

    def rows_sent(src, sems, to):
        for j in range(NX):
            for k in range(2):
                if j:
                    wait(src, sems.at[j, k])
                else:
                    pl.when(jnp.logical_not((yh == to) & (c == k)))(lambda k=k: wait(src, sems.at[0, k]))

    drains.append(lambda: rows_sent(va.at[my_slot, pl.ds(VB // 4, VB * 3 // 4)], s_vo.at[0], c))
    drains.append(lambda: rows_sent(va.at[my_slot, pl.ds(0, VB // 4)], s_vo.at[1], 1 - c))

    for d in range(1, NZ):
        wait(pr.at[d], r_p.at[0, d])
        wait(prs.at[d], r_p.at[1, d])
    levels = jnp.concatenate([prs[d, 0:1, :] for d in range(NZ)], axis=0)
    share = jnp.exp2(levels - jnp.max(levels, axis=0, keepdims=True))
    share = share / jnp.sum(share, axis=0, keepdims=True)
    share = jnp.transpose(jnp.concatenate([share, jnp.zeros((HD - NZ, HD), F32)], axis=0))
    mixed = share[:, 0:1] * pr[0].astype(F32)
    for d in range(1, NZ):
        mixed = mixed + share[:, d : d + 1] * pr[d].astype(F32)
    mixed = mixed.reshape(NX, 2, 2, 8, HD)
    for k in range(2):
        ao[k] = mixed[:, :, k].reshape(NX, 16, HD).astype(BF16)
    for j in range(NX):
        for k in range(2):
            copy = pltpu.make_async_remote_copy(
                src_ref=ao.at[k, (x + j) % NX], dst_ref=aa.at[my_slot], send_sem=s_ao.at[j, k], recv_sem=r_ao.at[my_slot],
                device_id=dev(c, (x + j) % NX, z, yl, k), device_id_type=MESH,
            )
            if j:
                copy.start()
            else:
                to_self = is_self & (c == k)

                @pl.when(to_self)
                def _(k=k):
                    pltpu.make_async_copy(ao.at[k, x], aa.at[my_slot], r_ao.at[my_slot]).start()

                @pl.when(jnp.logical_not(to_self))
                def _(copy=copy):
                    copy.start()

    drains.append(lambda: rows_sent(aa.at[my_slot], s_ao, c))

    for copy in own_w:
        copy.wait()
    for t, ref in enumerate((wv, wa)):
        wait(ref.at[1 - c], r_w.at[t])
    for h in range(2 * NX):
        wait(va.at[h, pl.ds(VB // 4, VB * 3 // 4)], r_vo.at[0, h])
        wait(va.at[h, pl.ds(0, VB // 4)], r_vo.at[1, h])
    xv = jnp.concatenate([va[h] for h in range(2 * NX)], axis=1)
    n_chunks = ysend.shape[0]
    width = ysend.shape[2]

    def y_copy(n, m):
        rows = pl.ds(m * VB // 4, VB // 4)
        return pltpu.make_async_remote_copy(
            src_ref=ysend.at[n, rows], dst_ref=yrecv.at[n, rows], send_sem=s_y.at[m, n], recv_sem=r_y.at[m, n],
            device_id=(cross_peer, yl_peer)[m], device_id_type=MESH,
        )

    def project(n, carry):
        at = pl.ds(pl.multiple_of(n * width, width), width)
        w = jnp.concatenate([wv[0, :, at], wv[1, :, at]], axis=0)
        y = jnp.dot(xv, w, preferred_element_type=F32)
        ysend[n] = y[: VB // 2].astype(BF16)
        yown[n] = y[VB // 2 :]
        for m in range(2):
            y_copy(n, m).start()
        return carry

    lax.fori_loop(0, n_chunks, project, 0)

    def y_sent():
        def one(n, carry):
            for m in range(2):
                y_copy(n, m).wait_send()
            return carry

        lax.fori_loop(0, n_chunks, one, 0)

    drains.append(y_sent)

    for h in range(2 * NX):
        wait(aa.at[h], r_ao.at[h])
    xa = jnp.concatenate([aa[h] for h in range(2 * NX)], axis=1)
    for n in range(wa.shape[2] // 512):
        at = slice(n * 512, (n + 1) * 512)
        w = jnp.concatenate([wa[0, :, at], wa[1, :, at]], axis=0)
        asend[:, :, at] = jnp.dot(xa, w, preferred_element_type=F32).reshape(2, 8, 512)
    last = pltpu.make_async_remote_copy(
        src_ref=asend.at[1 - yl], dst_ref=arecv, send_sem=s_ya, recv_sem=r_ya, device_id=yl_peer, device_id_type=MESH
    )
    last.start()
    drains.append(last.wait_send)

    def finish(n, carry):
        for m in range(2):
            y_copy(n, m).wait_recv()
        at = pl.ds(pl.multiple_of(n * width, width), width)
        ov[:, at] = (yown[n] + yrecv[n].astype(F32)).astype(BF16)
        return carry

    lax.fori_loop(0, n_chunks, finish, 0)

    last.wait_recv()
    oa[...] = (asend[yl] + arecv[...]).astype(BF16)

    for drain in drains:
        drain()


def hand_over(ov, oa, to_v, to_a):
    to_v[...] = ov[...]
    to_a[...] = oa[...]


def shards(vq, vk, vv, aq, ak, av, ws, wv, wa):
    n_chunks = 8
    dv, da = wv.shape[1], wa.shape[1]
    dma = pltpu.SemaphoreType.DMA
    vmem = pltpu.VMEM
    scratch = [
        vmem((NX, VR, HD), BF16),
        vmem((2, NX, VR, HD), BF16),
        vmem((2, NX, VR, HD), BF16),
        vmem((NZ, NX, AR, HD), BF16),
        vmem((2 * NX * NZ * AR // AB, AB, HD), BF16),
        vmem((2 * NX * NZ * AR // AB, AB, HD), BF16),
        vmem((2,) + wv.shape, BF16),
        vmem((2,) + wa.shape, BF16),
        vmem((2, NX, VR, HD), BF16),
        vmem((NX, 2, VB, HD), BF16),
        vmem((2 * NX, VB, HD), BF16),
        vmem((NZ, NX * AR, HD), BF16),
        vmem((NZ, 8, HD), F32),
        vmem((NZ, NX * AR, HD), BF16),
        vmem((NZ, 8, HD), F32),
        vmem((2, NX, 16, HD), BF16),
        vmem((2 * NX, 16, HD), BF16),
        vmem((n_chunks, VB // 2, dv // n_chunks), BF16),
        vmem((n_chunks, VB // 2, dv // n_chunks), BF16),
        vmem((n_chunks, VB // 2, dv // n_chunks), F32),
        vmem((2, 8, da), F32),
        vmem((8, da), F32),
        dma((3, NX)), dma((3, NX)),
        dma((3, NX)), dma((3, NX)),
        dma((2, 3, NZ // 2)), dma((2, 3, NZ // 2)),
        dma((2, NZ)), dma((2, NZ)),
        dma((2,)), dma((2,)),
        dma((2,)), dma((2,)),
        dma((2, NX, 2)), dma((2, 2 * NX)),
        dma((2, NZ)), dma((2, NZ)),
        dma((NX, 2)), dma((2 * NX,)),
        dma((2, n_chunks)), dma((2, n_chunks)),
        dma, dma,
        dma((2,)),
    ]
    any_spec = pl.BlockSpec(memory_space=pl.ANY)
    outs = pl.pallas_call(
        kernel,
        out_shape=(
            jax.ShapeDtypeStruct((vq.shape[0] // 4, dv), BF16),
            jax.ShapeDtypeStruct((aq.shape[0] // 4, da), BF16),
        ),
        in_specs=[pl.BlockSpec(memory_space=pltpu.SMEM)] + [any_spec] * 8,
        out_specs=(pl.BlockSpec(memory_space=pltpu.VMEM), pl.BlockSpec(memory_space=pltpu.VMEM)),
        scratch_shapes=scratch,
        compiler_params=pltpu.CompilerParams(
            collective_id=0, has_side_effects=True, vmem_limit_bytes=60 * 1024 * 1024
        ),
        cost_estimate=pl.CostEstimate(flops=3_000_000_000, bytes_accessed=16_000_000, transcendentals=4_000_000),
    )(ws, vq, vk, vv, aq, ak, av, wv, wa)
    return pl.pallas_call(
        hand_over, out_shape=tuple(jax.ShapeDtypeStruct(o.shape, o.dtype) for o in outs)
    )(*outs)


def solution(mesh):
    part = P("seq", "head")
    in_specs = (part, part, part, part, part, part, P(), P("head", None), P("head", None))
    out_specs = (P(("seq", "head"), None), P(("seq", "head"), None))
    return jax.shard_map(shards, mesh=mesh, in_specs=in_specs, out_specs=out_specs, check_vma=False)
```

```python
import math

import jax
import jax.numpy as jnp
from jax import lax
from jax.experimental import pallas as pl
from jax.experimental.pallas import tpu as pltpu
from jax.sharding import PartitionSpec as P

HD = 128
VB = 128
AB = 16
WIN = 80
NX, NZ = 4, 8
VR = 256
AR = 32
NEG = -1e30
C2 = math.log2(math.e) / math.sqrt(HD)
MESH = pl.DeviceIdType.MESH
F32, BF16 = jnp.float32, jnp.bfloat16


def dev(yh, x, z, yl, c):
    return ((yh * NX + x) * NZ + z, yl * 2 + c)


def nt(a, b):
    return lax.dot_general(a, b, (((1,), (1,)), ((), ())), preferred_element_type=F32)


def kernel(
    ws, vq_in, vk_in, vv_in, aq_in, ak_in, av_in, wv_in, wa_in, ov, oa,
    vq, vk, vv, aq, ak_flat, av_flat, wv, wa, kb, vo, va, po, pst, pr, prs, ao, aa, ysend, yrecv, yown, asend, arecv,
    s_pa, r_pa, s_pb, r_pb, s_z, r_z, s_f, r_f, s_vf, r_vf, s_w, r_w, s_vo, r_vo, s_p, r_p, s_ao, r_ao, s_y, r_y, s_ya, r_ya, l_w,
):
    seq, head = lax.axis_index("seq"), lax.axis_index("head")
    yh, x, z = seq // (NX * NZ), (seq // NZ) % NX, seq % NZ
    yl, c = head // 2, head % 2
    ak, av = (ref.reshape(2 * NX, NZ, AR, HD) for ref in (ak_flat, av_flat))
    is_self = yh == c
    core_peer = dev(yh, x, z, yl, 1 - c)
    yl_peer = dev(yh, x, z, 1 - yl, c)
    cross_peer = dev(1 - yh, x, z, 1 - yl, c)

    def peer(j):
        return dev(c, (x + j) % NX, z, yl, yh)

    drains = []

    def wait(ref, sem):
        pltpu.make_async_copy(ref, ref, sem).wait()

    own_w = [
        pltpu.make_async_copy(wv_in, wv.at[c], l_w.at[0]),
        pltpu.make_async_copy(wa_in, wa.at[c], l_w.at[1]),
    ]
    for copy in own_w:
        copy.start()

    barrier = pltpu.get_barrier_semaphore()

    def greet(device):
        pl.semaphore_signal(barrier, inc=1, device_id=device, device_id_type=MESH)

    group = [(p, j, q) for p in range(2) for j in range(NX) for q in range(2) if p or j or q]
    for p, j, q in group:
        greet(dev((yh + p) % 2, (x + j) % NX, z, yl, (c + q) % 2))
    for d in range(1, NZ):
        greet(dev(yh, x, (z + d) % NZ, yl, c))
    greet(yl_peer)
    greet(cross_peer)
    pl.semaphore_wait(barrier, len(group) + NZ + 1)

    other_w = [
        pltpu.make_async_remote_copy(
            src_ref=src, dst_ref=dst.at[c], send_sem=s_w.at[t], recv_sem=r_w.at[t],
            device_id=core_peer, device_id_type=MESH,
        )
        for t, (src, dst) in enumerate(((wv_in, wv), (wa_in, wa)))
    ]
    for copy in other_w:
        copy.start()

    drains.extend(copy.wait_send for copy in other_w)

    def exchange(src, dst, send, recv, j):
        remote = pltpu.make_async_remote_copy(
            src_ref=src, dst_ref=dst, send_sem=send, recv_sem=recv, device_id=peer(j), device_id_type=MESH
        )
        if j:
            remote.start()
            return

        @pl.when(is_self)
        def _():
            pltpu.make_async_copy(src, dst, recv).start()

        @pl.when(jnp.logical_not(is_self))
        def _():
            remote.start()

    def cols(j):
        return pl.ds(pl.multiple_of(((x + j) % NX) * HD, HD), HD)

    here = yh * NX + x
    for j in range(NX):
        exchange(aq_in.at[:, cols(j)], aq.at[z, x], s_pa.at[0, j], r_pa.at[0, x], j)
        exchange(ak_in.at[:, cols(j)], ak.at[here, z], s_pa.at[1, j], r_pa.at[1, x], j)
        exchange(av_in.at[:, cols(j)], av.at[here, z], s_pa.at[2, j], r_pa.at[2, x], j)
    def audio_sent(j):
        for t in range(3):
            wait(aq.at[z, x], s_pa.at[t, j])

    for j in range(1, NX):
        audio_sent(j)
    pl.when(jnp.logical_not(is_self))(lambda: audio_sent(0))
    for t, (src, dst) in enumerate(((vk_in, vk.at[yh]), (vv_in, vv.at[yh]), (vq_in, vq))):
        for j in range(NX):
            exchange(src.at[:, cols(j)], dst.at[x], s_pb.at[t, j], r_pb.at[t, x], j)

    def exchange_sent():
        def one(j):
            for t in range(3):
                wait(vq.at[x], s_pb.at[t, j])

        for j in range(1, NX):
            one(j)
        pl.when(jnp.logical_not(is_self))(lambda: one(0))

    drains.append(exchange_sent)

    lane = lax.broadcasted_iota(jnp.int32, (VB, 128), 1)
    for a in range(2):
        for xs in range(NX):
            for i in range(2):
                start = ws[((a * NX + xs) * NZ + z) * 2 + i]
                inside = (lane >= start) & (lane < start + WIN)
                kb[a, xs, pl.ds(i * VB, VB), :] = jnp.where(inside, 0.0, NEG).astype(BF16)

    for xs in range(NX):
        wait(aq.at[z, xs], r_pa.at[0, xs])
        wait(ak.at[c * NX + xs, z], r_pa.at[1, xs])
        wait(av.at[c * NX + xs, z], r_pa.at[2, xs])

    half = pl.ds(c * NX, NX)
    other_half = pl.ds((1 - c) * NX, NX)

    def chunk(t, zz):
        return aq.at[zz] if t == 0 else (ak, av)[t - 1].at[half, zz]

    def forward(t, zz):
        pltpu.make_async_remote_copy(
            src_ref=chunk(t, zz), dst_ref=chunk(t, zz), send_sem=s_f.at[t - 1, zz], recv_sem=r_f.at[t - 1, zz],
            device_id=core_peer, device_id_type=MESH,
        ).start()

    vf = []

    def share_video():
        for t, ref in enumerate((vk, vv)):
            for xs in range(NX):
                wait(ref.at[c, xs], r_pb.at[t, xs])
            copy = pltpu.make_async_remote_copy(
                src_ref=ref.at[c], dst_ref=ref.at[c], send_sem=s_vf.at[t], recv_sem=r_vf.at[t],
                device_id=core_peer, device_id_type=MESH,
            )
            copy.start()
            vf.append(copy)

    def hop_copy(way, t, k):
        zz = (z - k + 1 + NZ) % NZ if way == 0 else (z + k - 1) % NZ
        to = (z + 1) % NZ if way == 0 else (z + NZ - 1) % NZ
        return pltpu.make_async_remote_copy(
            src_ref=chunk(t, zz), dst_ref=chunk(t, zz), send_sem=s_z.at[way, t, k - 1], recv_sem=r_z.at[way, t, k - 1],
            device_id=dev(yh, x, to, yl, c), device_id_type=MESH,
        )

    def arrived(way, t, k):
        zz = (z - k + NZ) % NZ if way == 0 else (z + k) % NZ
        wait(chunk(t, zz), r_z.at[way, t, k - 1])
        if t:
            forward(t, zz)

    last_hops = [(0, 1), (1, 2), (0, 0)]

    def hops(k):
        return last_hops if k == NZ // 2 else [(way, t) for t in (1, 2, 0) for way in range(2)]

    def hop(k):
        for t in (1, 2, 0):
            for way in range(2):
                if k > 1:
                    arrived(way, t, k - 1)
                elif t and way == 0:
                    forward(t, z)
                if (way, t) in hops(k):
                    hop_copy(way, t, k).start()

    for k in range(1, NZ // 2):
        hop(k)
    share_video()

    def gather_end():
        for way, t in last_hops:
            arrived(way, t, NZ // 2)

    def gather_sent():
        for k in range(1, NZ // 2 + 1):
            for way, t in hops(k):
                hop_copy(way, t, k).wait_send()

        def one(zz, carry):
            wait(ak.at[half, zz], s_f.at[0, zz])
            wait(av.at[half, zz], s_f.at[1, zz])
            return carry

        lax.fori_loop(0, NZ, one, 0)

    drains.append(gather_sent)

    drains.extend(copy.wait_send for copy in vf)

    for t, ref in enumerate((vk, vv)):
        wait(ref.at[1 - c], r_vf.at[t])
    row = lax.broadcasted_iota(jnp.int32, (2 * NX * AR, 128), 0)
    lane2 = lax.broadcasted_iota(jnp.int32, (2 * NX * AR, 128), 1)
    x_of, b_of, u_of = (row // AR) % NX, (row % AR) // AB, row // (NX * AR)
    eye = lax.broadcasted_iota(jnp.int32, (HD, HD), 0) == lax.broadcasted_iota(jnp.int32, (HD, HD), 1)
    ones_vid = jnp.ones((2 * NX * VR, HD), BF16)

    def audio_pair(n, carry):
        pl.when(n == 1)(lambda: hop(NZ // 2))
        pl.when(n == NZ // 2 - 1)(gather_end)
        d0 = (n + 1) % (NZ // 2)
        d1 = jnp.where(d0 == 0, NZ // 2, NZ - d0)
        z0, z1 = (z + d0) % NZ, (z + d1) % NZ
        q = jnp.concatenate([aq[z0].reshape(NX * AR, HD), aq[z1].reshape(NX * AR, HD)], axis=0)
        zz = jnp.where(u_of == 0, z0, z1)
        block = ((c * NX + x_of) * NZ + zz) * 2 + b_of
        q = jnp.concatenate([q, jnp.where(lane2 == block, 1.0, 0.0).astype(BF16)], axis=1)
        key = jnp.concatenate([vk[...].reshape(2 * NX * VR, HD), kb[...].reshape(2 * NX * VR, HD)], axis=1)
        s = nt(q, key)
        top = jnp.max(s, axis=1, keepdims=True)
        p = jnp.exp2((s - top) * C2).astype(BF16)
        v = jnp.concatenate([vv[...].reshape(2 * NX * VR, HD), ones_vid], axis=1)
        o = jnp.dot(p, v, preferred_element_type=F32)
        part = (o[:, :HD] / o[:, HD:]).astype(BF16)
        level = top * C2 + jnp.log2(o[:, HD:])
        for u in range(2):
            d = d1 if u else d0
            rows = slice(u * NX * AR, (u + 1) * NX * AR)
            flat = jnp.sum(jnp.where(eye, level[rows], 0.0), axis=0, keepdims=True)
            flat = jnp.broadcast_to(flat, (8, HD))

            def keep(d=d, rows=rows, flat=flat):
                po[d] = part[rows]
                pst[d] = flat
                slot = NZ - d
                to = dev(yh, x, (z + d) % NZ, yl, c)
                for t, (src, dst) in enumerate(((po, pr), (pst, prs))):
                    pltpu.make_async_remote_copy(
                        src_ref=src.at[d], dst_ref=dst.at[slot], send_sem=s_p.at[t, d], recv_sem=r_p.at[t, slot],
                        device_id=to, device_id_type=MESH,
                    ).start()

            if u:
                keep()
            else:

                @pl.when(d == 0)
                def _(rows=rows, flat=flat):
                    pr[0] = part[rows]
                    prs[0] = flat

                pl.when(d > 0)(keep)
        return carry

    lax.fori_loop(0, NZ // 2, audio_pair, 0)

    def parts_sent():
        for d in range(1, NZ):
            wait(po.at[d], s_p.at[0, d])
            wait(pst.at[d], s_p.at[1, d])

    drains.append(parts_sent)
    for xs in range(NX):
        wait(vq.at[xs], r_pb.at[2, xs])

    def late(zz, carry):
        wait(ak.at[other_half, zz], r_f.at[0, zz])
        wait(av.at[other_half, zz], r_f.at[1, zz])
        return carry

    lax.fori_loop(0, NZ, late, 0)

    ones_win = jnp.ones((WIN * AB, HD), BF16)

    my_slot = yh * NX + x

    def send_rows(xs, j, k, m, to, rows):
        src, dst, recv = vo.at[xs, k, rows], va.at[my_slot, rows], r_vo.at[m, my_slot]
        to_self = (j == 0) & (yh == to) & (c == k)

        @pl.when(to_self)
        def _():
            pltpu.make_async_copy(src, dst, recv).start()

        @pl.when(jnp.logical_not(to_self))
        def _():
            pltpu.make_async_remote_copy(
                src_ref=src, dst_ref=dst, send_sem=s_vo.at[m, j, k], recv_sem=recv,
                device_id=dev(to, xs, z, yl, k), device_id_type=MESH,
            ).start()

    parts = ((1 - c, pl.ds(0, VB // 4)), (c, pl.ds(VB // 4, VB // 4)), (c, pl.ds(VB // 2, VB // 2)))

    def video_rows(n, carry):
        j = (n + 2) % NX
        xs = (x + j) % NX
        own = n // NX
        i = jnp.where(own == 1, yl, 1 - yl)
        start = ws[((c * NX + xs) * NZ + z) * 2 + i]
        blocks = pl.ds(start, WIN)
        s = nt(vq[xs, pl.ds(pl.multiple_of(i * VB, VB), VB), :], ak_flat[blocks].reshape(WIN * AB, HD))
        top = jnp.max(s, axis=1, keepdims=True)
        p = jnp.exp2((s - top) * C2).astype(BF16)
        v = jnp.concatenate([av_flat[blocks].reshape(WIN * AB, HD), ones_win], axis=1)
        o = jnp.dot(p, v, preferred_element_type=F32)
        o = (o[:, :HD] / o[:, HD:]).astype(BF16)
        at = pl.ds(pl.multiple_of(own * (VB // 2), VB // 2), VB // 2)
        for k in range(2):
            vo[xs, k, at, :] = o[k * VB // 2 : (k + 1) * VB // 2]

        @pl.when(own == 0)
        def _():
            for k in range(2):
                for m in range(2):
                    send_rows(xs, j, k, m, *parts[m])

        @pl.when(own == 1)
        def _():
            for k in range(2):
                send_rows(xs, j, k, 2, *parts[2])

        return carry

    lax.fori_loop(0, 2 * NX, video_rows, 0)

    def rows_sent(src, sems, to):
        for j in range(NX):
            for k in range(2):
                if j:
                    wait(src, sems.at[j, k])
                else:
                    pl.when(jnp.logical_not((yh == to) & (c == k)))(lambda k=k: wait(src, sems.at[0, k]))

    for m, (to, rows) in enumerate(parts):
        drains.append(lambda m=m, to=to, rows=rows: rows_sent(va.at[my_slot, rows], s_vo.at[m], to))

    for d in range(1, NZ):
        wait(pr.at[d], r_p.at[0, d])
        wait(prs.at[d], r_p.at[1, d])
    levels = jnp.concatenate([prs[d, 0:1, :] for d in range(NZ)], axis=0)
    share = jnp.exp2(levels - jnp.max(levels, axis=0, keepdims=True))
    share = share / jnp.sum(share, axis=0, keepdims=True)
    share = jnp.transpose(jnp.concatenate([share, jnp.zeros((HD - NZ, HD), F32)], axis=0))
    mixed = share[:, 0:1] * pr[0].astype(F32)
    for d in range(1, NZ):
        mixed = mixed + share[:, d : d + 1] * pr[d].astype(F32)
    mixed = mixed.reshape(NX, 2, 2, 8, HD)
    for k in range(2):
        ao[k] = mixed[:, :, k].reshape(NX, 16, HD).astype(BF16)
    for j in range(NX):
        for k in range(2):
            copy = pltpu.make_async_remote_copy(
                src_ref=ao.at[k, (x + j) % NX], dst_ref=aa.at[my_slot], send_sem=s_ao.at[j, k], recv_sem=r_ao.at[my_slot],
                device_id=dev(c, (x + j) % NX, z, yl, k), device_id_type=MESH,
            )
            if j:
                copy.start()
            else:
                to_self = is_self & (c == k)

                @pl.when(to_self)
                def _(k=k):
                    pltpu.make_async_copy(ao.at[k, x], aa.at[my_slot], r_ao.at[my_slot]).start()

                @pl.when(jnp.logical_not(to_self))
                def _(copy=copy):
                    copy.start()

    drains.append(lambda: rows_sent(aa.at[my_slot], s_ao, c))

    for copy in own_w:
        copy.wait()
    for t, ref in enumerate((wv, wa)):
        wait(ref.at[1 - c], r_w.at[t])

    def rows_here(*which):
        for h in range(2 * NX):
            for m in which:
                wait(va.at[h, parts[m][1]], r_vo.at[m, h])
        at = slice(0, VB // 2) if 0 in which else slice(VB // 2, VB)
        return jnp.concatenate([va[h, at, :] for h in range(2 * NX)], axis=1)

    n_chunks = ysend.shape[0]
    width = ysend.shape[2]

    def y_copy(n, m):
        rows = pl.ds(m * VB // 4, VB // 4)
        return pltpu.make_async_remote_copy(
            src_ref=ysend.at[n, rows], dst_ref=yrecv.at[n, rows], send_sem=s_y.at[m, n], recv_sem=r_y.at[m, n],
            device_id=(cross_peer, yl_peer)[m], device_id_type=MESH,
        )

    def project(x_rows, n):
        at = pl.ds(pl.multiple_of(n * width, width), width)
        w = jnp.concatenate([wv[0, :, at], wv[1, :, at]], axis=0)
        return jnp.dot(x_rows, w, preferred_element_type=F32)

    x_other = rows_here(0, 1)

    def project_other(n, carry):
        ysend[n] = project(x_other, n).astype(BF16)
        for m in range(2):
            y_copy(n, m).start()
        return carry

    lax.fori_loop(0, n_chunks, project_other, 0)

    x_own = rows_here(2)

    def project_own(n, carry):
        yown[n] = project(x_own, n)
        return carry

    lax.fori_loop(0, n_chunks, project_own, 0)

    def y_sent():
        def one(n, carry):
            for m in range(2):
                y_copy(n, m).wait_send()
            return carry

        lax.fori_loop(0, n_chunks, one, 0)


    for h in range(2 * NX):
        wait(aa.at[h], r_ao.at[h])
    xa = jnp.concatenate([aa[h] for h in range(2 * NX)], axis=1)
    for n in range(wa.shape[2] // 512):
        at = slice(n * 512, (n + 1) * 512)
        w = jnp.concatenate([wa[0, :, at], wa[1, :, at]], axis=0)
        asend[:, :, at] = jnp.dot(xa, w, preferred_element_type=F32).reshape(2, 8, 512)
    last = pltpu.make_async_remote_copy(
        src_ref=asend.at[1 - yl], dst_ref=arecv, send_sem=s_ya, recv_sem=r_ya, device_id=yl_peer, device_id_type=MESH
    )
    last.start()

    for drain in drains:
        drain()

    def finish(n, carry):
        for m in range(2):
            y_copy(n, m).wait_recv()
        at = pl.ds(pl.multiple_of(n * width, width), width)
        ov[:, at] = (yown[n] + yrecv[n].astype(F32)).astype(BF16)
        return carry

    lax.fori_loop(0, n_chunks, finish, 0)

    last.wait_recv()
    oa[...] = (asend[yl] + arecv[...]).astype(BF16)

    last.wait_send()
    y_sent()


def hand_over(ov, oa, to_v, to_a):
    to_v[...] = ov[...]
    to_a[...] = oa[...]


def shards(vq, vk, vv, aq, ak, av, ws, wv, wa):
    n_chunks = 8
    dv, da = wv.shape[1], wa.shape[1]
    dma = pltpu.SemaphoreType.DMA
    vmem = pltpu.VMEM
    scratch = [
        vmem((NX, VR, HD), BF16),
        vmem((2, NX, VR, HD), BF16),
        vmem((2, NX, VR, HD), BF16),
        vmem((NZ, NX, AR, HD), BF16),
        vmem((2 * NX * NZ * AR // AB, AB, HD), BF16),
        vmem((2 * NX * NZ * AR // AB, AB, HD), BF16),
        vmem((2,) + wv.shape, BF16),
        vmem((2,) + wa.shape, BF16),
        vmem((2, NX, VR, HD), BF16),
        vmem((NX, 2, VB, HD), BF16),
        vmem((2 * NX, VB, HD), BF16),
        vmem((NZ, NX * AR, HD), BF16),
        vmem((NZ, 8, HD), F32),
        vmem((NZ, NX * AR, HD), BF16),
        vmem((NZ, 8, HD), F32),
        vmem((2, NX, 16, HD), BF16),
        vmem((2 * NX, 16, HD), BF16),
        vmem((n_chunks, VB // 2, dv // n_chunks), BF16),
        vmem((n_chunks, VB // 2, dv // n_chunks), BF16),
        vmem((n_chunks, VB // 2, dv // n_chunks), F32),
        vmem((2, 8, da), F32),
        vmem((8, da), F32),
        dma((3, NX)), dma((3, NX)),
        dma((3, NX)), dma((3, NX)),
        dma((2, 3, NZ // 2)), dma((2, 3, NZ // 2)),
        dma((2, NZ)), dma((2, NZ)),
        dma((2,)), dma((2,)),
        dma((2,)), dma((2,)),
        dma((3, NX, 2)), dma((3, 2 * NX)),
        dma((2, NZ)), dma((2, NZ)),
        dma((NX, 2)), dma((2 * NX,)),
        dma((2, n_chunks)), dma((2, n_chunks)),
        dma, dma,
        dma((2,)),
    ]
    any_spec = pl.BlockSpec(memory_space=pl.ANY)
    outs = pl.pallas_call(
        kernel,
        out_shape=(
            jax.ShapeDtypeStruct((vq.shape[0] // 4, dv), BF16),
            jax.ShapeDtypeStruct((aq.shape[0] // 4, da), BF16),
        ),
        in_specs=[pl.BlockSpec(memory_space=pltpu.SMEM)] + [any_spec] * 8,
        out_specs=(pl.BlockSpec(memory_space=pltpu.VMEM), pl.BlockSpec(memory_space=pltpu.VMEM)),
        scratch_shapes=scratch,
        compiler_params=pltpu.CompilerParams(
            collective_id=0, has_side_effects=True, vmem_limit_bytes=60 * 1024 * 1024
        ),
        cost_estimate=pl.CostEstimate(flops=3_000_000_000, bytes_accessed=16_000_000, transcendentals=4_000_000),
    )(ws, vq, vk, vv, aq, ak, av, wv, wa)
    return pl.pallas_call(
        hand_over, out_shape=tuple(jax.ShapeDtypeStruct(o.shape, o.dtype) for o in outs)
    )(*outs)


def solution(mesh):
    part = P("seq", "head")
    in_specs = (part, part, part, part, part, part, P(), P("head", None), P("head", None))
    out_specs = (P(("seq", "head"), None), P(("seq", "head"), None))
    return jax.shard_map(shards, mesh=mesh, in_specs=in_specs, out_specs=out_specs, check_vma=False)
```

```python
import math

import jax
import jax.numpy as jnp
from jax import lax
from jax.experimental import pallas as pl
from jax.experimental.pallas import tpu as pltpu
from jax.sharding import PartitionSpec as P

HD = 128
VB = 128
AB = 16
WIN = 80
NX, NZ = 4, 8
VR = 256
AR = 32
NEG = -1e30
C2 = math.log2(math.e) / math.sqrt(HD)
MESH = pl.DeviceIdType.MESH
F32, BF16 = jnp.float32, jnp.bfloat16


def dev(yh, x, z, yl, c):
    return ((yh * NX + x) * NZ + z, yl * 2 + c)


def nt(a, b):
    return lax.dot_general(a, b, (((1,), (1,)), ((), ())), preferred_element_type=F32)


def kernel(
    ws, vq_in, vk_in, vv_in, aq_in, ak_in, av_in, wv_in, wa_in, ov, oa,
    vq, vk, vv, aq, ak_flat, av_flat, wv, wa, kb, vo, va, po, pst, pr, prs, ao, aa, ysend, yrecv, yown, aown, asend, arecv,
    s_pa, r_pa, s_pb, r_pb, s_z, r_z, s_f, r_f, s_vf, r_vf, s_w, r_w, s_vo, r_vo, s_p, r_p, s_ao, r_ao, s_y, r_y, s_ya, r_ya, l_w,
):
    seq, head = lax.axis_index("seq"), lax.axis_index("head")
    yh, x, z = seq // (NX * NZ), (seq // NZ) % NX, seq % NZ
    yl, c = head // 2, head % 2
    ak, av = (ref.reshape(2 * NX, NZ, AR, HD) for ref in (ak_flat, av_flat))
    is_self = yh == c
    core_peer = dev(yh, x, z, yl, 1 - c)
    yl_peer = dev(yh, x, z, 1 - yl, c)
    cross_peer = dev(1 - yh, x, z, 1 - yl, c)

    def peer(j):
        return dev(c, (x + j) % NX, z, yl, yh)

    drains = []

    def wait(ref, sem):
        pltpu.make_async_copy(ref, ref, sem).wait()

    own_w = [
        pltpu.make_async_copy(wv_in, wv.at[c], l_w.at[0]),
        pltpu.make_async_copy(wa_in, wa.at[c], l_w.at[1]),
    ]
    for copy in own_w:
        copy.start()

    barrier = pltpu.get_barrier_semaphore()

    def greet(device):
        pl.semaphore_signal(barrier, inc=1, device_id=device, device_id_type=MESH)

    group = [(p, j, q) for p in range(2) for j in range(NX) for q in range(2) if p or j or q]
    for p, j, q in group:
        greet(dev((yh + p) % 2, (x + j) % NX, z, yl, (c + q) % 2))
    for d in range(1, NZ):
        greet(dev(yh, x, (z + d) % NZ, yl, c))
    greet(yl_peer)
    greet(cross_peer)
    pl.semaphore_wait(barrier, len(group) + NZ + 1)

    other_w = [
        pltpu.make_async_remote_copy(
            src_ref=src, dst_ref=dst.at[c], send_sem=s_w.at[t], recv_sem=r_w.at[t],
            device_id=core_peer, device_id_type=MESH,
        )
        for t, (src, dst) in enumerate(((wv_in, wv), (wa_in, wa)))
    ]
    for copy in other_w:
        copy.start()

    drains.extend(copy.wait_send for copy in other_w)

    def exchange(src, dst, send, recv, j):
        remote = pltpu.make_async_remote_copy(
            src_ref=src, dst_ref=dst, send_sem=send, recv_sem=recv, device_id=peer(j), device_id_type=MESH
        )
        if j:
            remote.start()
            return

        @pl.when(is_self)
        def _():
            pltpu.make_async_copy(src, dst, recv).start()

        @pl.when(jnp.logical_not(is_self))
        def _():
            remote.start()

    def cols(j):
        return pl.ds(pl.multiple_of(((x + j) % NX) * HD, HD), HD)

    here = yh * NX + x
    for j in range(NX):
        exchange(aq_in.at[:, cols(j)], aq.at[z, x], s_pa.at[0, j], r_pa.at[0, x], j)
        exchange(ak_in.at[:, cols(j)], ak.at[here, z], s_pa.at[1, j], r_pa.at[1, x], j)
        exchange(av_in.at[:, cols(j)], av.at[here, z], s_pa.at[2, j], r_pa.at[2, x], j)
    def audio_sent(j):
        for t in range(3):
            wait(aq.at[z, x], s_pa.at[t, j])

    for j in range(1, NX):
        audio_sent(j)
    pl.when(jnp.logical_not(is_self))(lambda: audio_sent(0))
    for t, (src, dst) in enumerate(((vk_in, vk.at[yh]), (vv_in, vv.at[yh]), (vq_in, vq))):
        for j in range(NX):
            exchange(src.at[:, cols(j)], dst.at[x], s_pb.at[t, j], r_pb.at[t, x], j)

    def exchange_sent():
        def one(j):
            for t in range(3):
                wait(vq.at[x], s_pb.at[t, j])

        for j in range(1, NX):
            one(j)
        pl.when(jnp.logical_not(is_self))(lambda: one(0))

    drains.append(exchange_sent)

    lane = lax.broadcasted_iota(jnp.int32, (VB, 128), 1)
    for a in range(2):
        for xs in range(NX):
            for i in range(2):
                start = ws[((a * NX + xs) * NZ + z) * 2 + i]
                inside = (lane >= start) & (lane < start + WIN)
                kb[a, xs, pl.ds(i * VB, VB), :] = jnp.where(inside, 0.0, NEG).astype(BF16)

    for xs in range(NX):
        wait(aq.at[z, xs], r_pa.at[0, xs])
        wait(ak.at[c * NX + xs, z], r_pa.at[1, xs])
        wait(av.at[c * NX + xs, z], r_pa.at[2, xs])

    half = pl.ds(c * NX, NX)
    other_half = pl.ds((1 - c) * NX, NX)

    def chunk(t, zz):
        return aq.at[zz] if t == 0 else (ak, av)[t - 1].at[half, zz]

    def forward(t, zz):
        pltpu.make_async_remote_copy(
            src_ref=chunk(t, zz), dst_ref=chunk(t, zz), send_sem=s_f.at[t - 1, zz], recv_sem=r_f.at[t - 1, zz],
            device_id=core_peer, device_id_type=MESH,
        ).start()

    vf = []

    def share_video():
        for t, ref in enumerate((vk, vv)):
            for xs in range(NX):
                wait(ref.at[c, xs], r_pb.at[t, xs])
            copy = pltpu.make_async_remote_copy(
                src_ref=ref.at[c], dst_ref=ref.at[c], send_sem=s_vf.at[t], recv_sem=r_vf.at[t],
                device_id=core_peer, device_id_type=MESH,
            )
            copy.start()
            vf.append(copy)

    def hop_copy(way, t, k):
        zz = (z - k + 1 + NZ) % NZ if way == 0 else (z + k - 1) % NZ
        to = (z + 1) % NZ if way == 0 else (z + NZ - 1) % NZ
        return pltpu.make_async_remote_copy(
            src_ref=chunk(t, zz), dst_ref=chunk(t, zz), send_sem=s_z.at[way, t, k - 1], recv_sem=r_z.at[way, t, k - 1],
            device_id=dev(yh, x, to, yl, c), device_id_type=MESH,
        )

    def arrived(way, t, k):
        zz = (z - k + NZ) % NZ if way == 0 else (z + k) % NZ
        wait(chunk(t, zz), r_z.at[way, t, k - 1])
        if t:
            forward(t, zz)

    last_hops = [(0, 1), (1, 2), (0, 0)]

    def hops(k):
        return last_hops if k == NZ // 2 else [(way, t) for t in (1, 2, 0) for way in range(2)]

    def hop(k):
        for t in (1, 2, 0):
            for way in range(2):
                if k > 1:
                    arrived(way, t, k - 1)
                elif t and way == 0:
                    forward(t, z)
                if (way, t) in hops(k):
                    hop_copy(way, t, k).start()

    for k in range(1, NZ // 2):
        hop(k)
    share_video()

    def gather_end():
        for way, t in last_hops:
            arrived(way, t, NZ // 2)

    def gather_sent():
        for k in range(1, NZ // 2 + 1):
            for way, t in hops(k):
                hop_copy(way, t, k).wait_send()

        def one(zz, carry):
            wait(ak.at[half, zz], s_f.at[0, zz])
            wait(av.at[half, zz], s_f.at[1, zz])
            return carry

        lax.fori_loop(0, NZ, one, 0)

    drains.append(gather_sent)

    drains.extend(copy.wait_send for copy in vf)

    for t, ref in enumerate((vk, vv)):
        wait(ref.at[1 - c], r_vf.at[t])
    row = lax.broadcasted_iota(jnp.int32, (2 * NX * AR, 128), 0)
    lane2 = lax.broadcasted_iota(jnp.int32, (2 * NX * AR, 128), 1)
    x_of, b_of, u_of = (row // AR) % NX, (row % AR) // AB, row // (NX * AR)
    eye = lax.broadcasted_iota(jnp.int32, (HD, HD), 0) == lax.broadcasted_iota(jnp.int32, (HD, HD), 1)
    ones_vid = jnp.ones((2 * NX * VR, HD), BF16)

    def audio_pair(n, carry):
        pl.when(n == 1)(lambda: hop(NZ // 2))
        pl.when(n == NZ // 2 - 1)(gather_end)
        d0 = (n + 1) % (NZ // 2)
        d1 = jnp.where(d0 == 0, NZ // 2, NZ - d0)
        z0, z1 = (z + d0) % NZ, (z + d1) % NZ
        q = jnp.concatenate([aq[z0].reshape(NX * AR, HD), aq[z1].reshape(NX * AR, HD)], axis=0)
        zz = jnp.where(u_of == 0, z0, z1)
        block = ((c * NX + x_of) * NZ + zz) * 2 + b_of
        q = jnp.concatenate([q, jnp.where(lane2 == block, 1.0, 0.0).astype(BF16)], axis=1)
        key = jnp.concatenate([vk[...].reshape(2 * NX * VR, HD), kb[...].reshape(2 * NX * VR, HD)], axis=1)
        s = nt(q, key)
        top = jnp.max(s, axis=1, keepdims=True)
        p = jnp.exp2((s - top) * C2).astype(BF16)
        v = jnp.concatenate([vv[...].reshape(2 * NX * VR, HD), ones_vid], axis=1)
        o = jnp.dot(p, v, preferred_element_type=F32)
        part = (o[:, :HD] / o[:, HD:]).astype(BF16)
        level = top * C2 + jnp.log2(o[:, HD:])
        for u in range(2):
            d = d1 if u else d0
            rows = slice(u * NX * AR, (u + 1) * NX * AR)
            flat = jnp.sum(jnp.where(eye, level[rows], 0.0), axis=0, keepdims=True)
            flat = jnp.broadcast_to(flat, (8, HD))

            def keep(d=d, rows=rows, flat=flat):
                po[d] = part[rows]
                pst[d] = flat
                slot = NZ - d
                to = dev(yh, x, (z + d) % NZ, yl, c)
                for t, (src, dst) in enumerate(((po, pr), (pst, prs))):
                    pltpu.make_async_remote_copy(
                        src_ref=src.at[d], dst_ref=dst.at[slot], send_sem=s_p.at[t, d], recv_sem=r_p.at[t, slot],
                        device_id=to, device_id_type=MESH,
                    ).start()

            if u:
                keep()
            else:

                @pl.when(d == 0)
                def _(rows=rows, flat=flat):
                    pr[0] = part[rows]
                    prs[0] = flat

                pl.when(d > 0)(keep)
        return carry

    lax.fori_loop(0, NZ // 2, audio_pair, 0)

    def parts_sent():
        for d in range(1, NZ):
            wait(po.at[d], s_p.at[0, d])
            wait(pst.at[d], s_p.at[1, d])

    drains.append(parts_sent)
    for xs in range(NX):
        wait(vq.at[xs], r_pb.at[2, xs])

    def late(zz, carry):
        wait(ak.at[other_half, zz], r_f.at[0, zz])
        wait(av.at[other_half, zz], r_f.at[1, zz])
        return carry

    lax.fori_loop(0, NZ, late, 0)

    ones_win = jnp.ones((WIN * AB, HD), BF16)

    my_slot = yh * NX + x

    def send_rows(xs, j, k, m, to, rows):
        src, dst, recv = vo.at[xs, k, rows], va.at[my_slot, rows], r_vo.at[m, my_slot]
        to_self = (j == 0) & (yh == to) & (c == k)

        @pl.when(to_self)
        def _():
            pltpu.make_async_copy(src, dst, recv).start()

        @pl.when(jnp.logical_not(to_self))
        def _():
            pltpu.make_async_remote_copy(
                src_ref=src, dst_ref=dst, send_sem=s_vo.at[m, j, k], recv_sem=recv,
                device_id=dev(to, xs, z, yl, k), device_id_type=MESH,
            ).start()

    parts = ((1 - c, pl.ds(0, VB // 4)), (c, pl.ds(VB // 4, VB // 4)), (c, pl.ds(VB // 2, VB // 2)))

    def video_rows(n, carry):
        j = (n + 2) % NX
        xs = (x + j) % NX
        own = n // NX
        i = jnp.where(own == 1, yl, 1 - yl)
        start = ws[((c * NX + xs) * NZ + z) * 2 + i]
        blocks = pl.ds(start, WIN)
        s = nt(vq[xs, pl.ds(pl.multiple_of(i * VB, VB), VB), :], ak_flat[blocks].reshape(WIN * AB, HD))
        top = jnp.max(s, axis=1, keepdims=True)
        p = jnp.exp2((s - top) * C2).astype(BF16)
        v = jnp.concatenate([av_flat[blocks].reshape(WIN * AB, HD), ones_win], axis=1)
        o = jnp.dot(p, v, preferred_element_type=F32)
        o = (o[:, :HD] / o[:, HD:]).astype(BF16)
        at = pl.ds(pl.multiple_of(own * (VB // 2), VB // 2), VB // 2)
        for k in range(2):
            vo[xs, k, at, :] = o[k * VB // 2 : (k + 1) * VB // 2]

        @pl.when(own == 0)
        def _():
            for k in range(2):
                for m in range(2):
                    send_rows(xs, j, k, m, *parts[m])

        @pl.when(own == 1)
        def _():
            for k in range(2):
                send_rows(xs, j, k, 2, *parts[2])

        return carry

    lax.fori_loop(0, 2 * NX, video_rows, 0)

    for d in range(1, NZ):
        wait(pr.at[d], r_p.at[0, d])
        wait(prs.at[d], r_p.at[1, d])
    levels = jnp.concatenate([prs[d, 0:1, :] for d in range(NZ)], axis=0)
    share = jnp.exp2(levels - jnp.max(levels, axis=0, keepdims=True))
    share = share / jnp.sum(share, axis=0, keepdims=True)
    share = jnp.transpose(jnp.concatenate([share, jnp.zeros((HD - NZ, HD), F32)], axis=0))
    mixed = share[:, 0:1] * pr[0].astype(F32)
    for d in range(1, NZ):
        mixed = mixed + share[:, d : d + 1] * pr[d].astype(F32)
    mixed = mixed.reshape(NX, 2, 2, 8, HD)
    for k in range(2):
        ao[k] = mixed[:, :, k].reshape(NX, 16, HD).astype(BF16)
    for j in range(NX):
        for k in range(2):
            copy = pltpu.make_async_remote_copy(
                src_ref=ao.at[k, (x + j) % NX], dst_ref=aa.at[my_slot], send_sem=s_ao.at[j, k], recv_sem=r_ao.at[my_slot],
                device_id=dev(c, (x + j) % NX, z, yl, k), device_id_type=MESH,
            )
            if j:
                copy.start()
            else:
                to_self = is_self & (c == k)

                @pl.when(to_self)
                def _(k=k):
                    pltpu.make_async_copy(ao.at[k, x], aa.at[my_slot], r_ao.at[my_slot]).start()

                @pl.when(jnp.logical_not(to_self))
                def _(copy=copy):
                    copy.start()

    drains.append(lambda: rows_sent(aa.at[my_slot], s_ao, c))

    def rows_sent(src, sems, to):
        for j in range(NX):
            for k in range(2):
                if j:
                    wait(src, sems.at[j, k])
                else:
                    pl.when(jnp.logical_not((yh == to) & (c == k)))(lambda k=k: wait(src, sems.at[0, k]))

    for m, (to, rows) in enumerate(parts):
        drains.append(lambda m=m, to=to, rows=rows: rows_sent(va.at[my_slot, rows], s_vo.at[m], to))

    for copy in own_w:
        copy.wait()
    for t, ref in enumerate((wv, wa)):
        wait(ref.at[1 - c], r_w.at[t])

    def rows_here(*which):
        for h in range(2 * NX):
            for m in which:
                wait(va.at[h, parts[m][1]], r_vo.at[m, h])
        at = slice(0, VB // 2) if 0 in which else slice(VB // 2, VB)
        return jnp.concatenate([va[h, at, :] for h in range(2 * NX)], axis=1)

    n_chunks = ysend.shape[0]
    width = ysend.shape[2]

    def y_copy(n, m):
        rows = pl.ds(m * VB // 4, VB // 4)
        return pltpu.make_async_remote_copy(
            src_ref=ysend.at[n, rows], dst_ref=yrecv.at[n, rows], send_sem=s_y.at[m, n], recv_sem=r_y.at[m, n],
            device_id=(cross_peer, yl_peer)[m], device_id_type=MESH,
        )

    def project(x_rows, n):
        at = pl.ds(pl.multiple_of(n * width, width), width)
        w = jnp.concatenate([wv[0, :, at], wv[1, :, at]], axis=0)
        return jnp.dot(x_rows, w, preferred_element_type=F32)

    x_other = rows_here(0, 1)

    def project_other(n, carry):
        ysend[n] = project(x_other, n).astype(BF16)
        for m in range(2):
            y_copy(n, m).start()
        return carry

    lax.fori_loop(0, n_chunks, project_other, 0)

    for h in range(2 * NX):
        wait(aa.at[h], r_ao.at[h])
    xa = jnp.concatenate([aa[h] for h in range(2 * NX)], axis=1)
    for n in range(wa.shape[2] // 512):
        at = slice(n * 512, (n + 1) * 512)
        w = jnp.concatenate([wa[0, :, at], wa[1, :, at]], axis=0)
        y = jnp.dot(xa, w, preferred_element_type=F32).reshape(2, 8, 512)
        aown[:, :, at] = y
        side = n * 1024 // wa.shape[2]
        at = slice(n * 512 - side * wa.shape[2] // 2, (n + 1) * 512 - side * wa.shape[2] // 2)
        asend[:, 8 * side : 8 * side + 8, at] = y.astype(BF16)
    last = pltpu.make_async_remote_copy(
        src_ref=asend.at[1 - yl], dst_ref=arecv, send_sem=s_ya, recv_sem=r_ya, device_id=yl_peer, device_id_type=MESH
    )
    last.start()

    x_own = rows_here(2)

    def project_own(n, carry):
        yown[n] = project(x_own, n)
        return carry

    lax.fori_loop(0, n_chunks, project_own, 0)

    def y_sent():
        def one(n, carry):
            for m in range(2):
                y_copy(n, m).wait_send()
            return carry

        lax.fori_loop(0, n_chunks, one, 0)


    for drain in drains:
        drain()

    def finish(n, carry):
        for m in range(2):
            y_copy(n, m).wait_recv()
        at = pl.ds(pl.multiple_of(n * width, width), width)
        ov[:, at] = (yown[n] + yrecv[n].astype(F32)).astype(BF16)
        return carry

    lax.fori_loop(0, n_chunks, finish, 0)

    last.wait_recv()
    theirs = arecv[...].astype(F32)
    oa[...] = (aown[yl] + jnp.concatenate([theirs[:8], theirs[8:]], axis=1)).astype(BF16)

    last.wait_send()
    y_sent()


def hand_over(ov, oa, to_v, to_a):
    to_v[...] = ov[...]
    to_a[...] = oa[...]


def shards(vq, vk, vv, aq, ak, av, ws, wv, wa):
    n_chunks = 8
    dv, da = wv.shape[1], wa.shape[1]
    dma = pltpu.SemaphoreType.DMA
    vmem = pltpu.VMEM
    scratch = [
        vmem((NX, VR, HD), BF16),
        vmem((2, NX, VR, HD), BF16),
        vmem((2, NX, VR, HD), BF16),
        vmem((NZ, NX, AR, HD), BF16),
        vmem((2 * NX * NZ * AR // AB, AB, HD), BF16),
        vmem((2 * NX * NZ * AR // AB, AB, HD), BF16),
        vmem((2,) + wv.shape, BF16),
        vmem((2,) + wa.shape, BF16),
        vmem((2, NX, VR, HD), BF16),
        vmem((NX, 2, VB, HD), BF16),
        vmem((2 * NX, VB, HD), BF16),
        vmem((NZ, NX * AR, HD), BF16),
        vmem((NZ, 8, HD), F32),
        vmem((NZ, NX * AR, HD), BF16),
        vmem((NZ, 8, HD), F32),
        vmem((2, NX, 16, HD), BF16),
        vmem((2 * NX, 16, HD), BF16),
        vmem((n_chunks, VB // 2, dv // n_chunks), BF16),
        vmem((n_chunks, VB // 2, dv // n_chunks), BF16),
        vmem((n_chunks, VB // 2, dv // n_chunks), F32),
        vmem((2, 8, da), F32),
        vmem((2, 16, da // 2), BF16),
        vmem((16, da // 2), BF16),
        dma((3, NX)), dma((3, NX)),
        dma((3, NX)), dma((3, NX)),
        dma((2, 3, NZ // 2)), dma((2, 3, NZ // 2)),
        dma((2, NZ)), dma((2, NZ)),
        dma((2,)), dma((2,)),
        dma((2,)), dma((2,)),
        dma((3, NX, 2)), dma((3, 2 * NX)),
        dma((2, NZ)), dma((2, NZ)),
        dma((NX, 2)), dma((2 * NX,)),
        dma((2, n_chunks)), dma((2, n_chunks)),
        dma, dma,
        dma((2,)),
    ]
    any_spec = pl.BlockSpec(memory_space=pl.ANY)
    outs = pl.pallas_call(
        kernel,
        out_shape=(
            jax.ShapeDtypeStruct((vq.shape[0] // 4, dv), BF16),
            jax.ShapeDtypeStruct((aq.shape[0] // 4, da), BF16),
        ),
        in_specs=[pl.BlockSpec(memory_space=pltpu.SMEM)] + [any_spec] * 8,
        out_specs=(pl.BlockSpec(memory_space=pltpu.VMEM), pl.BlockSpec(memory_space=pltpu.VMEM)),
        scratch_shapes=scratch,
        compiler_params=pltpu.CompilerParams(
            collective_id=0, has_side_effects=True, vmem_limit_bytes=60 * 1024 * 1024
        ),
        cost_estimate=pl.CostEstimate(flops=3_000_000_000, bytes_accessed=16_000_000, transcendentals=4_000_000),
    )(ws, vq, vk, vv, aq, ak, av, wv, wa)
    return pl.pallas_call(
        hand_over, out_shape=tuple(jax.ShapeDtypeStruct(o.shape, o.dtype) for o in outs)
    )(*outs)


def solution(mesh):
    part = P("seq", "head")
    in_specs = (part, part, part, part, part, part, P(), P("head", None), P("head", None))
    out_specs = (P(("seq", "head"), None), P(("seq", "head"), None))
    return jax.shard_map(shards, mesh=mesh, in_specs=in_specs, out_specs=out_specs, check_vma=False)
```

```python
import math

import jax
import jax.numpy as jnp
from jax import lax
from jax.experimental import pallas as pl
from jax.experimental.pallas import tpu as pltpu
from jax.sharding import PartitionSpec as P

HD = 128
VB = 128
AB = 16
WIN = 80
NX, NZ = 4, 8
VR = 256
AR = 32
NEG = -1e30
C2 = math.log2(math.e) / math.sqrt(HD)
MESH = pl.DeviceIdType.MESH
F32, BF16 = jnp.float32, jnp.bfloat16


def dev(yh, x, z, yl, c):
    return ((yh * NX + x) * NZ + z, yl * 2 + c)


def nt(a, b):
    return lax.dot_general(a, b, (((1,), (1,)), ((), ())), preferred_element_type=F32)


def kernel(
    ws, vq_in, vk_in, vv_in, aq_in, ak_in, av_in, wv_in, wa_in, ov, oa,
    vq, vk, vv, aq, ak_flat, av_flat, wv, wa, kb, vo, va, po, pst, pr, prs, ao, aa, ysend, yrecv, yown, aown, asend, arecv,
    s_pa, r_pa, s_pb, r_pb, s_z, r_z, s_f, r_f, s_vf, r_vf, s_w, r_w, s_vo, r_vo, s_p, r_p, s_ao, r_ao, s_y, r_y, s_ya, r_ya, l_w, ov_held, l_o,
):
    seq, head = lax.axis_index("seq"), lax.axis_index("head")
    yh, x, z = seq // (NX * NZ), (seq // NZ) % NX, seq % NZ
    yl, c = head // 2, head % 2
    ak, av = (ref.reshape(2 * NX, NZ, AR, HD) for ref in (ak_flat, av_flat))
    is_self = yh == c
    core_peer = dev(yh, x, z, yl, 1 - c)
    yl_peer = dev(yh, x, z, 1 - yl, c)
    cross_peer = dev(1 - yh, x, z, 1 - yl, c)

    def peer(j):
        return dev(c, (x + j) % NX, z, yl, yh)

    drains = []

    def wait(ref, sem):
        pltpu.make_async_copy(ref, ref, sem).wait()

    own_w = [
        pltpu.make_async_copy(wv_in, wv.at[c], l_w.at[0]),
        pltpu.make_async_copy(wa_in, wa.at[c], l_w.at[1]),
    ]
    for copy in own_w:
        copy.start()

    barrier = pltpu.get_barrier_semaphore()

    def greet(device):
        pl.semaphore_signal(barrier, inc=1, device_id=device, device_id_type=MESH)

    group = [(p, j, q) for p in range(2) for j in range(NX) for q in range(2) if p or j or q]
    for p, j, q in group:
        greet(dev((yh + p) % 2, (x + j) % NX, z, yl, (c + q) % 2))
    for d in range(1, NZ):
        greet(dev(yh, x, (z + d) % NZ, yl, c))
    greet(yl_peer)
    greet(cross_peer)
    pl.semaphore_wait(barrier, len(group) + NZ + 1)

    other_w = [
        pltpu.make_async_remote_copy(
            src_ref=src, dst_ref=dst.at[c], send_sem=s_w.at[t], recv_sem=r_w.at[t],
            device_id=core_peer, device_id_type=MESH,
        )
        for t, (src, dst) in enumerate(((wv_in, wv), (wa_in, wa)))
    ]
    for copy in other_w:
        copy.start()

    drains.extend(copy.wait_send for copy in other_w)

    def exchange(src, dst, send, recv, j):
        remote = pltpu.make_async_remote_copy(
            src_ref=src, dst_ref=dst, send_sem=send, recv_sem=recv, device_id=peer(j), device_id_type=MESH
        )
        if j:
            remote.start()
            return

        @pl.when(is_self)
        def _():
            pltpu.make_async_copy(src, dst, recv).start()

        @pl.when(jnp.logical_not(is_self))
        def _():
            remote.start()

    def cols(j):
        return pl.ds(pl.multiple_of(((x + j) % NX) * HD, HD), HD)

    here = yh * NX + x
    for j in range(NX):
        exchange(aq_in.at[:, cols(j)], aq.at[z, x], s_pa.at[0, j], r_pa.at[0, x], j)
        exchange(ak_in.at[:, cols(j)], ak.at[here, z], s_pa.at[1, j], r_pa.at[1, x], j)
        exchange(av_in.at[:, cols(j)], av.at[here, z], s_pa.at[2, j], r_pa.at[2, x], j)
    def audio_sent(j):
        for t in range(3):
            wait(aq.at[z, x], s_pa.at[t, j])

    for j in range(1, NX):
        audio_sent(j)
    pl.when(jnp.logical_not(is_self))(lambda: audio_sent(0))
    for t, (src, dst) in enumerate(((vk_in, vk.at[yh]), (vv_in, vv.at[yh]), (vq_in, vq))):
        for j in range(NX):
            exchange(src.at[:, cols(j)], dst.at[x], s_pb.at[t, j], r_pb.at[t, x], j)

    def exchange_sent():
        def one(j):
            for t in range(3):
                wait(vq.at[x], s_pb.at[t, j])

        for j in range(1, NX):
            one(j)
        pl.when(jnp.logical_not(is_self))(lambda: one(0))

    drains.append(exchange_sent)

    lane = lax.broadcasted_iota(jnp.int32, (VB, 128), 1)
    for a in range(2):
        for xs in range(NX):
            for i in range(2):
                start = ws[((a * NX + xs) * NZ + z) * 2 + i]
                inside = (lane >= start) & (lane < start + WIN)
                kb[a, xs, pl.ds(i * VB, VB), :] = jnp.where(inside, 0.0, NEG).astype(BF16)

    for xs in range(NX):
        wait(aq.at[z, xs], r_pa.at[0, xs])
        wait(ak.at[c * NX + xs, z], r_pa.at[1, xs])
        wait(av.at[c * NX + xs, z], r_pa.at[2, xs])

    half = pl.ds(c * NX, NX)
    other_half = pl.ds((1 - c) * NX, NX)

    def chunk(t, zz):
        return aq.at[zz] if t == 0 else (ak, av)[t - 1].at[half, zz]

    def forward(t, zz):
        pltpu.make_async_remote_copy(
            src_ref=chunk(t, zz), dst_ref=chunk(t, zz), send_sem=s_f.at[t - 1, zz], recv_sem=r_f.at[t - 1, zz],
            device_id=core_peer, device_id_type=MESH,
        ).start()

    vf = []

    def share_video():
        for t, ref in enumerate((vk, vv)):
            for xs in range(NX):
                wait(ref.at[c, xs], r_pb.at[t, xs])
            copy = pltpu.make_async_remote_copy(
                src_ref=ref.at[c], dst_ref=ref.at[c], send_sem=s_vf.at[t], recv_sem=r_vf.at[t],
                device_id=core_peer, device_id_type=MESH,
            )
            copy.start()
            vf.append(copy)

    def hop_copy(way, t, k):
        zz = (z - k + 1 + NZ) % NZ if way == 0 else (z + k - 1) % NZ
        to = (z + 1) % NZ if way == 0 else (z + NZ - 1) % NZ
        return pltpu.make_async_remote_copy(
            src_ref=chunk(t, zz), dst_ref=chunk(t, zz), send_sem=s_z.at[way, t, k - 1], recv_sem=r_z.at[way, t, k - 1],
            device_id=dev(yh, x, to, yl, c), device_id_type=MESH,
        )

    def arrived(way, t, k):
        zz = (z - k + NZ) % NZ if way == 0 else (z + k) % NZ
        wait(chunk(t, zz), r_z.at[way, t, k - 1])
        if t:
            forward(t, zz)

    last_hops = [(0, 1), (1, 2), (0, 0)]

    def hops(k):
        return last_hops if k == NZ // 2 else [(way, t) for t in (1, 2, 0) for way in range(2)]

    def hop(k):
        for t in (1, 2, 0):
            for way in range(2):
                if k > 1:
                    arrived(way, t, k - 1)
                elif t and way == 0:
                    forward(t, z)
                if (way, t) in hops(k):
                    hop_copy(way, t, k).start()

    for k in range(1, NZ // 2):
        hop(k)
    share_video()

    def gather_end():
        for way, t in last_hops:
            arrived(way, t, NZ // 2)

    def gather_sent():
        for k in range(1, NZ // 2 + 1):
            for way, t in hops(k):
                hop_copy(way, t, k).wait_send()

        def one(zz, carry):
            wait(ak.at[half, zz], s_f.at[0, zz])
            wait(av.at[half, zz], s_f.at[1, zz])
            return carry

        lax.fori_loop(0, NZ, one, 0)

    drains.append(gather_sent)

    drains.extend(copy.wait_send for copy in vf)

    for t, ref in enumerate((vk, vv)):
        wait(ref.at[1 - c], r_vf.at[t])
    row = lax.broadcasted_iota(jnp.int32, (2 * NX * AR, 128), 0)
    lane2 = lax.broadcasted_iota(jnp.int32, (2 * NX * AR, 128), 1)
    x_of, b_of, u_of = (row // AR) % NX, (row % AR) // AB, row // (NX * AR)
    eye = lax.broadcasted_iota(jnp.int32, (HD, HD), 0) == lax.broadcasted_iota(jnp.int32, (HD, HD), 1)
    ones_vid = jnp.ones((2 * NX * VR, HD), BF16)

    def audio_pair(n, carry):
        pl.when(n == 1)(lambda: hop(NZ // 2))
        pl.when(n == NZ // 2 - 1)(gather_end)
        d0 = (n + 1) % (NZ // 2)
        d1 = jnp.where(d0 == 0, NZ // 2, NZ - d0)
        z0, z1 = (z + d0) % NZ, (z + d1) % NZ
        q = jnp.concatenate([aq[z0].reshape(NX * AR, HD), aq[z1].reshape(NX * AR, HD)], axis=0)
        zz = jnp.where(u_of == 0, z0, z1)
        block = ((c * NX + x_of) * NZ + zz) * 2 + b_of
        q = jnp.concatenate([q, jnp.where(lane2 == block, 1.0, 0.0).astype(BF16)], axis=1)
        key = jnp.concatenate([vk[...].reshape(2 * NX * VR, HD), kb[...].reshape(2 * NX * VR, HD)], axis=1)
        s = nt(q, key)
        top = jnp.max(s, axis=1, keepdims=True)
        p = jnp.exp2((s - top) * C2).astype(BF16)
        v = jnp.concatenate([vv[...].reshape(2 * NX * VR, HD), ones_vid], axis=1)
        o = jnp.dot(p, v, preferred_element_type=F32)
        part = (o[:, :HD] / o[:, HD:]).astype(BF16)
        level = top * C2 + jnp.log2(o[:, HD:])
        for u in range(2):
            d = d1 if u else d0
            rows = slice(u * NX * AR, (u + 1) * NX * AR)
            flat = jnp.sum(jnp.where(eye, level[rows], 0.0), axis=0, keepdims=True)
            flat = jnp.broadcast_to(flat, (8, HD))

            def keep(d=d, rows=rows, flat=flat):
                po[d] = part[rows]
                pst[d] = flat
                slot = NZ - d
                to = dev(yh, x, (z + d) % NZ, yl, c)
                for t, (src, dst) in enumerate(((po, pr), (pst, prs))):
                    pltpu.make_async_remote_copy(
                        src_ref=src.at[d], dst_ref=dst.at[slot], send_sem=s_p.at[t, d], recv_sem=r_p.at[t, slot],
                        device_id=to, device_id_type=MESH,
                    ).start()

            if u:
                keep()
            else:

                @pl.when(d == 0)
                def _(rows=rows, flat=flat):
                    pr[0] = part[rows]
                    prs[0] = flat

                pl.when(d > 0)(keep)
        return carry

    lax.fori_loop(0, NZ // 2, audio_pair, 0)

    def parts_sent():
        for d in range(1, NZ):
            wait(po.at[d], s_p.at[0, d])
            wait(pst.at[d], s_p.at[1, d])

    drains.append(parts_sent)
    for xs in range(NX):
        wait(vq.at[xs], r_pb.at[2, xs])

    def late(zz, carry):
        wait(ak.at[other_half, zz], r_f.at[0, zz])
        wait(av.at[other_half, zz], r_f.at[1, zz])
        return carry

    lax.fori_loop(0, NZ, late, 0)

    ones_win = jnp.ones((WIN * AB, HD), BF16)

    my_slot = yh * NX + x

    def send_rows(xs, j, k, m, to, rows):
        src, dst, recv = vo.at[xs, k, rows], va.at[my_slot, rows], r_vo.at[m, my_slot]
        to_self = (j == 0) & (yh == to) & (c == k)

        @pl.when(to_self)
        def _():
            pltpu.make_async_copy(src, dst, recv).start()

        @pl.when(jnp.logical_not(to_self))
        def _():
            pltpu.make_async_remote_copy(
                src_ref=src, dst_ref=dst, send_sem=s_vo.at[m, j, k], recv_sem=recv,
                device_id=dev(to, xs, z, yl, k), device_id_type=MESH,
            ).start()

    parts = ((1 - c, pl.ds(0, VB // 4)), (c, pl.ds(VB // 4, VB // 4)), (c, pl.ds(VB // 2, VB // 2)))

    def video_rows(n, carry):
        j = (n + 2) % NX
        xs = (x + j) % NX
        own = n // NX
        i = jnp.where(own == 1, yl, 1 - yl)
        start = ws[((c * NX + xs) * NZ + z) * 2 + i]
        blocks = pl.ds(start, WIN)
        s = nt(vq[xs, pl.ds(pl.multiple_of(i * VB, VB), VB), :], ak_flat[blocks].reshape(WIN * AB, HD))
        top = jnp.max(s, axis=1, keepdims=True)
        p = jnp.exp2((s - top) * C2).astype(BF16)
        v = jnp.concatenate([av_flat[blocks].reshape(WIN * AB, HD), ones_win], axis=1)
        o = jnp.dot(p, v, preferred_element_type=F32)
        o = (o[:, :HD] / o[:, HD:]).astype(BF16)
        at = pl.ds(pl.multiple_of(own * (VB // 2), VB // 2), VB // 2)
        for k in range(2):
            vo[xs, k, at, :] = o[k * VB // 2 : (k + 1) * VB // 2]

        @pl.when(own == 0)
        def _():
            for k in range(2):
                for m in range(2):
                    send_rows(xs, j, k, m, *parts[m])

        @pl.when(own == 1)
        def _():
            for k in range(2):
                send_rows(xs, j, k, 2, *parts[2])

        return carry

    lax.fori_loop(0, 2 * NX, video_rows, 0)

    for d in range(1, NZ):
        wait(pr.at[d], r_p.at[0, d])
        wait(prs.at[d], r_p.at[1, d])
    levels = jnp.concatenate([prs[d, 0:1, :] for d in range(NZ)], axis=0)
    share = jnp.exp2(levels - jnp.max(levels, axis=0, keepdims=True))
    share = share / jnp.sum(share, axis=0, keepdims=True)
    share = jnp.transpose(jnp.concatenate([share, jnp.zeros((HD - NZ, HD), F32)], axis=0))
    mixed = share[:, 0:1] * pr[0].astype(F32)
    for d in range(1, NZ):
        mixed = mixed + share[:, d : d + 1] * pr[d].astype(F32)
    mixed = mixed.reshape(NX, 2, 2, 8, HD)
    for k in range(2):
        ao[k] = mixed[:, :, k].reshape(NX, 16, HD).astype(BF16)
    for j in range(NX):
        for k in range(2):
            copy = pltpu.make_async_remote_copy(
                src_ref=ao.at[k, (x + j) % NX], dst_ref=aa.at[my_slot], send_sem=s_ao.at[j, k], recv_sem=r_ao.at[my_slot],
                device_id=dev(c, (x + j) % NX, z, yl, k), device_id_type=MESH,
            )
            if j:
                copy.start()
            else:
                to_self = is_self & (c == k)

                @pl.when(to_self)
                def _(k=k):
                    pltpu.make_async_copy(ao.at[k, x], aa.at[my_slot], r_ao.at[my_slot]).start()

                @pl.when(jnp.logical_not(to_self))
                def _(copy=copy):
                    copy.start()

    drains.append(lambda: rows_sent(aa.at[my_slot], s_ao, c))

    def rows_sent(src, sems, to):
        for j in range(NX):
            for k in range(2):
                if j:
                    wait(src, sems.at[j, k])
                else:
                    pl.when(jnp.logical_not((yh == to) & (c == k)))(lambda k=k: wait(src, sems.at[0, k]))

    for m, (to, rows) in enumerate(parts):
        drains.append(lambda m=m, to=to, rows=rows: rows_sent(va.at[my_slot, rows], s_vo.at[m], to))

    for copy in own_w:
        copy.wait()
    for t, ref in enumerate((wv, wa)):
        wait(ref.at[1 - c], r_w.at[t])

    def rows_here(*which):
        for h in range(2 * NX):
            for m in which:
                wait(va.at[h, parts[m][1]], r_vo.at[m, h])
        at = slice(0, VB // 2) if 0 in which else slice(VB // 2, VB)
        return jnp.concatenate([va[h, at, :] for h in range(2 * NX)], axis=1)

    n_chunks = ysend.shape[0]
    width = ysend.shape[2]

    def y_copy(n, m):
        rows = pl.ds(m * VB // 4, VB // 4)
        return pltpu.make_async_remote_copy(
            src_ref=ysend.at[n, rows], dst_ref=yrecv.at[n, rows], send_sem=s_y.at[m, n], recv_sem=r_y.at[m, n],
            device_id=(cross_peer, yl_peer)[m], device_id_type=MESH,
        )

    def project(x_rows, n):
        at = pl.ds(pl.multiple_of(n * width, width), width)
        w = jnp.concatenate([wv[0, :, at], wv[1, :, at]], axis=0)
        return jnp.dot(x_rows, w, preferred_element_type=F32)

    x_other = rows_here(0, 1)

    def project_other(n, carry):
        ysend[n] = project(x_other, n).astype(BF16)
        for m in range(2):
            y_copy(n, m).start()
        return carry

    lax.fori_loop(0, n_chunks, project_other, 0)

    for h in range(2 * NX):
        wait(aa.at[h], r_ao.at[h])
    xa = jnp.concatenate([aa[h] for h in range(2 * NX)], axis=1)
    for n in range(wa.shape[2] // 512):
        at = slice(n * 512, (n + 1) * 512)
        w = jnp.concatenate([wa[0, :, at], wa[1, :, at]], axis=0)
        y = jnp.dot(xa, w, preferred_element_type=F32).reshape(2, 8, 512)
        aown[:, :, at] = y
        side = n * 1024 // wa.shape[2]
        at = slice(n * 512 - side * wa.shape[2] // 2, (n + 1) * 512 - side * wa.shape[2] // 2)
        asend[:, 8 * side : 8 * side + 8, at] = y.astype(BF16)
    last = pltpu.make_async_remote_copy(
        src_ref=asend.at[1 - yl], dst_ref=arecv, send_sem=s_ya, recv_sem=r_ya, device_id=yl_peer, device_id_type=MESH
    )
    last.start()

    x_own = rows_here(2)

    def project_own(n, carry):
        yown[n] = project(x_own, n)
        return carry

    lax.fori_loop(0, n_chunks, project_own, 0)

    def y_sent():
        def one(n, carry):
            for m in range(2):
                y_copy(n, m).wait_send()
            return carry

        lax.fori_loop(0, n_chunks, one, 0)


    for drain in drains:
        drain()

    def ov_copy(n):
        at = pl.ds(pl.multiple_of(n * width, width), width)
        return pltpu.make_async_copy(ov_held.at[n], ov.at[:, at], l_o.at[n])

    def finish(n, carry):
        for m in range(2):
            y_copy(n, m).wait_recv()
        ov_held[n] = (yown[n] + yrecv[n].astype(F32)).astype(BF16)
        ov_copy(n).start()
        return carry

    lax.fori_loop(0, n_chunks, finish, 0)

    last.wait_recv()
    theirs = arecv[...].astype(F32)
    oa[...] = (aown[yl] + jnp.concatenate([theirs[:8], theirs[8:]], axis=1)).astype(BF16)

    def written(n, carry):
        ov_copy(n).wait()
        return carry

    lax.fori_loop(0, n_chunks, written, 0)

    last.wait_send()
    y_sent()


def hand_over(ov, oa, to_v, to_a, tv, ta, sems):
    rows = ov.shape[0] // 2
    steps = [(ov.at[pl.ds(i * rows, rows)], tv.at[pl.ds(i * rows, rows)], to_v.at[pl.ds(i * rows, rows)]) for i in range(2)]
    steps.append((oa, ta, to_a))
    ins = [pltpu.make_async_copy(src, held, sems.at[0, i]) for i, (src, held, _) in enumerate(steps)]
    outs = [pltpu.make_async_copy(held, dst, sems.at[1, i]) for i, (_, held, dst) in enumerate(steps)]
    for copy in ins:
        copy.start()
    for arrived, leave in zip(ins, outs):
        arrived.wait()
        leave.start()
    for copy in outs:
        copy.wait()


def shards(vq, vk, vv, aq, ak, av, ws, wv, wa):
    n_chunks = 8
    dv, da = wv.shape[1], wa.shape[1]
    dma = pltpu.SemaphoreType.DMA
    vmem = pltpu.VMEM
    scratch = [
        vmem((NX, VR, HD), BF16),
        vmem((2, NX, VR, HD), BF16),
        vmem((2, NX, VR, HD), BF16),
        vmem((NZ, NX, AR, HD), BF16),
        vmem((2 * NX * NZ * AR // AB, AB, HD), BF16),
        vmem((2 * NX * NZ * AR // AB, AB, HD), BF16),
        vmem((2,) + wv.shape, BF16),
        vmem((2,) + wa.shape, BF16),
        vmem((2, NX, VR, HD), BF16),
        vmem((NX, 2, VB, HD), BF16),
        vmem((2 * NX, VB, HD), BF16),
        vmem((NZ, NX * AR, HD), BF16),
        vmem((NZ, 8, HD), F32),
        vmem((NZ, NX * AR, HD), BF16),
        vmem((NZ, 8, HD), F32),
        vmem((2, NX, 16, HD), BF16),
        vmem((2 * NX, 16, HD), BF16),
        vmem((n_chunks, VB // 2, dv // n_chunks), BF16),
        vmem((n_chunks, VB // 2, dv // n_chunks), BF16),
        vmem((n_chunks, VB // 2, dv // n_chunks), F32),
        vmem((2, 8, da), F32),
        vmem((2, 16, da // 2), BF16),
        vmem((16, da // 2), BF16),
        dma((3, NX)), dma((3, NX)),
        dma((3, NX)), dma((3, NX)),
        dma((2, 3, NZ // 2)), dma((2, 3, NZ // 2)),
        dma((2, NZ)), dma((2, NZ)),
        dma((2,)), dma((2,)),
        dma((2,)), dma((2,)),
        dma((3, NX, 2)), dma((3, 2 * NX)),
        dma((2, NZ)), dma((2, NZ)),
        dma((NX, 2)), dma((2 * NX,)),
        dma((2, n_chunks)), dma((2, n_chunks)),
        dma, dma,
        dma((2,)),
        vmem((n_chunks, VB // 2, dv // n_chunks), BF16),
        dma((n_chunks,)),
    ]
    any_spec = pl.BlockSpec(memory_space=pl.ANY)
    outs = pl.pallas_call(
        kernel,
        out_shape=(
            jax.ShapeDtypeStruct((vq.shape[0] // 4, dv), BF16),
            jax.ShapeDtypeStruct((aq.shape[0] // 4, da), BF16),
        ),
        in_specs=[pl.BlockSpec(memory_space=pltpu.SMEM)] + [any_spec] * 8,
        out_specs=(any_spec, pl.BlockSpec(memory_space=pltpu.VMEM)),
        scratch_shapes=scratch,
        compiler_params=pltpu.CompilerParams(
            collective_id=0, has_side_effects=True, vmem_limit_bytes=60 * 1024 * 1024
        ),
        cost_estimate=pl.CostEstimate(flops=3_000_000_000, bytes_accessed=16_000_000, transcendentals=4_000_000),
    )(ws, vq, vk, vv, aq, ak, av, wv, wa)
    return pl.pallas_call(
        hand_over,
        out_shape=tuple(jax.ShapeDtypeStruct(o.shape, o.dtype) for o in outs),
        in_specs=[any_spec] * 2,
        out_specs=(any_spec, any_spec),
        scratch_shapes=[vmem(o.shape, o.dtype) for o in outs] + [dma((2, 3))],
    )(*outs)


def solution(mesh):
    part = P("seq", "head")
    in_specs = (part, part, part, part, part, part, P(), P("head", None), P("head", None))
    out_specs = (P(("seq", "head"), None), P(("seq", "head"), None))
    return jax.shard_map(shards, mesh=mesh, in_specs=in_specs, out_specs=out_specs, check_vma=False)
```
